512 devices in a mesh: col: 16 (over x, y), row: 32 (over z, core).
Axes of the slice: x: 4, y: 4, z: 16, core: 2. Of those that a mesh axis runs over, the one named last changes fastest.
Arguments:
- tile_values: bfloat16 [24576, 128, 128], P(('col', 'row')), may hold values from -0.0546875 to 0.0546875
- tile_row: int32 [24576], P(('col', 'row')), may hold values from 0 to 8, as said below
- tile_column: int32 [24576], P(('col', 'row')), may hold values from 0 to 15
- unit_cost: float32 [256, 128], P('col'), may hold values from -5 to 5
- capacity: float32 [256, 128], P('col'), may hold values from 0.3 to 3
- demand: float32 [256, 128, 128], P('row'), may hold values from -6 to 6
- row_kind: int32 [256, 128], P('row'), may hold values 0 or 1
- primal_start: float32 [256, 128, 128], P('col'), may hold values from 0 to 1.5
- dual_start: float32 [256, 128, 128], P('row'), may hold values from -6 to 6
Outputs:
- primal_final: float32 [256, 128, 128], P('col')
- dual_final: float32 [256, 128, 128], P('row')
The draws below stay inside these ranges and needn't reach their ends.
Inputs may be any that keep to these rules, and one draw needn't show every extreme that they name: The value 8 marks an empty slot; empty slots come after the live ones of a device; the live slots of one device name distinct pairs of tile_row and tile_column.
All inputs are finite; a program needn't handle non-finite values. No bound on the sum of `row_kind` on one device may be relied on, other than what follows from the above.
Results may differ from the reference program's by a relative error of at most 0.004.
Values sent between devices are 32-bit elements; how exact they have to be, the bound alone decides.
A program may use at most 64 MiB of HBM per device.

```python
import math
import jax
import jax.numpy as jnp
from jax import lax

TILE = 128
RB_DEV = 8
CB_DEV = 16
SLOTS = 48
S = 128
ITERS = 2
RBLOCKS = 256
CBLOCKS = 256
N_COL = 16
N_ROW = 32
DEVICES = 512


def slot_places(key):
    places = RB_DEV * CB_DEV
    position = jnp.arange(places, dtype=jnp.int32)
    scores = jax.random.randint(key, (DEVICES, places), 0, 1 << 20, dtype=jnp.int32) * places + position[None, :]
    scores = jnp.where(position[None, :] == 0, -2, scores)
    scores = jnp.where(position[None, :] == places - 1, -1, scores)
    order = jnp.argsort(scores, axis=1, stable=True).astype(jnp.int32)
    chosen = order[:, :SLOTS].reshape(DEVICES * SLOTS)
    return (chosen // CB_DEV, chosen % CB_DEV)


def live_counts():
    position = jnp.arange(DEVICES * SLOTS, dtype=jnp.int32)
    device = position // SLOTS
    slot = position % SLOTS
    section = device % N_ROW * 4 // N_ROW
    live = SLOTS - section * (SLOTS // 4)
    return (slot, live)


def draw_tile_row(key, part):
    rows_drawn, cols_drawn = slot_places(key)
    slot, live = live_counts()
    return jnp.where(slot < live, rows_drawn, RB_DEV).astype(jnp.int32)


def draw_tile_column(key, part):
    rows_drawn, cols_drawn = slot_places(key)
    return cols_drawn.astype(jnp.int32)


def with_ends(values, key, least, largest):
    dims = values.shape
    place = [jax.random.randint(jax.random.fold_in(key, axis), (), 0, dims[axis]) for axis in range(len(dims))]
    values = values.at[tuple(place)].set(least)
    longest = dims.index(max(dims))
    place[longest] = (place[longest] + 1) % dims[longest]
    return values.at[tuple(place)].set(largest)


def steps_of(stream_key, dims, pieces, low, largest):
    gain = 1.0
    for dim, blocks in pieces:
        draws = jax.random.uniform(jax.random.fold_in(jax.random.fold_in(stream_key, 6), dim), (blocks,), jnp.float32, low / len(pieces), largest / len(pieces))
        gain = gain * jnp.repeat(jnp.exp(draws), dims[dim] // blocks).reshape((-1,) + (1,) * (len(dims) - 1 - dim))
    return gain


def gaussian(key, extent, spread, most, shards=(), kind=jnp.bfloat16):
    result = jax.random.normal(key, extent, jnp.float32) * spread
    if len(shards) > 0:
        result = steps_of(key, extent, shards, -0.22, 0.18) * result
    return jnp.clip(result, min=-most, max=most).astype(kind)


def setup_inputs(seed: int = 0) -> dict:
    splits = jax.random.split(jax.random.key(seed), 10)
    return {
        "tile_values": gaussian(splits[0], (DEVICES * SLOTS, TILE, TILE), (TILE * N_ROW * SLOTS // CB_DEV) ** -0.5, 0.0546875, ((0, 512),)),
        "tile_row": draw_tile_row(jax.random.fold_in(splits[9], 71), 0),
        "tile_column": draw_tile_column(jax.random.fold_in(splits[9], 71), 0),
        "unit_cost": gaussian(splits[3], (CBLOCKS, TILE), 1.0, 5.0, ((0, 16),), jnp.float32),
        "capacity": jnp.clip(jnp.exp(math.log(3.0) - 2.3025851 * jax.random.uniform(splits[4], (CBLOCKS, TILE), jnp.float32) ** steps_of(splits[4], (CBLOCKS, TILE), ((0, 16),), -0.2, 0.2)), 0.3, 3.0),
        "demand": gaussian(splits[5], (RBLOCKS, TILE, S), 1.0, 6.0, ((0, 32),), jnp.float32),
        "row_kind": with_ends((jax.random.randint(splits[6], (RBLOCKS, TILE), 0, 4) < 3).astype(jnp.int32), jax.random.fold_in(splits[6], 1), 0, 1),
        "primal_start": jnp.clip(1.5 * jax.random.uniform(splits[7], (CBLOCKS, TILE, S), jnp.float32) ** steps_of(splits[7], (CBLOCKS, TILE, S), ((0, 16),), -0.2, 0.2), 0.0, 1.5),
        "dual_start": gaussian(splits[8], (RBLOCKS, TILE, S), 1.0, 6.0, ((0, 32),), jnp.float32),
    }


primal_step = 0.5
dual_step = 0.5


def apply_tiles(tile_values, tile_row, tile_column, source, forward):
    total_dev = N_COL * N_ROW
    if forward:
        accum = jnp.zeros((RBLOCKS, TILE, S), jnp.float32)
    else:
        accum = jnp.zeros((CBLOCKS, TILE, S), jnp.float32)

    def one_device(carry, device):
        start = (device * SLOTS).astype(jnp.int32)
        block = lax.dynamic_slice_in_dim(tile_values, start, SLOTS, 0).astype(jnp.float32)
        rows_here = lax.dynamic_slice_in_dim(tile_row, start, SLOTS, 0)
        cols_here = lax.dynamic_slice_in_dim(tile_column, start, SLOTS, 0)
        col_index = (device // N_ROW).astype(jnp.int32)
        row_index = (device % N_ROW).astype(jnp.int32)
        live = (rows_here < RB_DEV).astype(jnp.float32)
        global_row = (row_index * RB_DEV + jnp.minimum(rows_here, RB_DEV - 1)).astype(jnp.int32)
        global_col = (col_index * CB_DEV + cols_here).astype(jnp.int32)
        if forward:
            picked = source[global_col].astype(jnp.float32)
            product = jnp.einsum('tij,tjs->tis', block, picked) * live[:, None, None]
            carry = carry.at[global_row].add(product)
        else:
            picked = source[global_row].astype(jnp.float32)
            product = jnp.einsum('tij,tis->tjs', block, picked) * live[:, None, None]
            carry = carry.at[global_col].add(product)
        return carry, None

    accum, _ = lax.scan(one_device, accum, jnp.arange(total_dev, dtype=jnp.int32))
    return accum


def reference(tile_values, tile_row, tile_column, unit_cost, capacity, demand, row_kind, primal_start, dual_start):
    primal = primal_start
    dual = dual_start
    for iteration in range(ITERS):
        dual_low = dual.astype(jnp.bfloat16)
        adjoint = apply_tiles(tile_values, tile_row, tile_column, dual_low, False)
        primal_new = jnp.minimum(jnp.maximum(primal - primal_step * (unit_cost[:, :, None] - adjoint), 0.0), capacity[:, :, None])
        extrapolated = (2.0 * primal_new - primal).astype(jnp.bfloat16)
        forward = apply_tiles(tile_values, tile_row, tile_column, extrapolated, True)
        dual_new = dual + dual_step * (demand - forward)
        dual_new = jnp.where(row_kind[:, :, None] == 1, jnp.maximum(dual_new, 0.0), dual_new)
        primal = primal_new
        dual = dual_new
    return primal, dual
```

```python
import jax
import jax.numpy as jnp
from jax import lax
from jax.experimental import pallas as pl
from jax.experimental.pallas import tpu as pltpu
from jax.sharding import PartitionSpec as P

ITERS = 2
NX, NY, NZ = 4, 4, 16
RB, CB, T, S = 8, 16, 128, 128
H = S // 2
Q = 2
HQ = H // Q
FR = 32
SLOTS = 48

primal_step = 0.5
dual_step = 0.5


def kernel(
    inv_ref,
    tiles,
    cost,
    cap,
    demand,
    kind,
    primal0,
    dual0,
    primal_out,
    dual_out,
    kd,
    pt,
    dt,
    dl,
    ap,
    sib,
    rs_s,
    rs_r,
    fp,
    rx,
    g,
    ry,
    dem,
    ring_send,
    ring_recv,
    sib_send,
    sib_recv,
    f_send,
    f_recv,
):
    col = lax.axis_index("col")
    row = lax.axis_index("row")
    x, y = col // NY, col % NY
    z, core = row // 2, row % 2
    own = pl.multiple_of(core * H, H)
    oth = pl.multiple_of((1 - core) * H, H)

    def zdev(d):
        return (col, ((z + d + NZ) % NZ) * 2 + core)

    sibling = (col, z * 2 + 1 - core)

    def xdev(d):
        return (((x + d) % NX) * NY + y, row)

    def ydev(d):
        return (x * NY + (y + d) % NY, row)

    barrier = pltpu.get_barrier_semaphore()
    peers = [zdev(1), zdev(-1), sibling]
    peers += [xdev(d) for d in (1, 2, 3)] + [ydev(d) for d in (1, 2, 3)]
    for peer in peers:
        pl.semaphore_signal(
            barrier, inc=1, device_id=peer, device_id_type=pl.DeviceIdType.MESH
        )

    def place(p, _):
        idx = inv_ref[p]
        tile = tiles[jnp.maximum(idx, 0)].astype(jnp.float32)
        tile = jnp.where(idx >= 0, tile, 0.0).astype(jnp.bfloat16)
        r0 = pl.multiple_of((p // CB) * T, T)
        kd[p % CB, pl.ds(r0, T), :] = tile
        return 0

    lax.fori_loop(0, RB * CB, place, 0)
    for b in range(RB):
        dt[0, b] = dual0[b].T

    pl.semaphore_wait(barrier, len(peers))

    def remote(src, dst, ss, rs, dev):
        return pltpu.make_async_remote_copy(
            src_ref=src,
            dst_ref=dst,
            send_sem=ss,
            recv_sem=rs,
            device_id=dev,
            device_id_type=pl.DeviceIdType.MESH,
        )

    step_of = (1, -1)

    def rs_copy(it, d, t, q):
        i = (it, d, t - 1, q)
        return remote(
            rs_s.at[i], rs_r.at[i], ring_send.at[it, 0, d, t - 1, q],
            ring_recv.at[it, 0, d, t - 1, q], zdev(step_of[d]),
        )

    def ag_copy(it, d, t, q, c):
        part = pt.at[it + 1, c, pl.ds(own + q * HQ, HQ), :]
        return remote(
            part, part, ring_send.at[it, 1, d, t - 1, q],
            ring_recv.at[it, 1, d, t - 1, q], zdev(step_of[d]),
        )

    def sib_rs(it, c):
        return remote(
            ap.at[it, c, pl.ds(oth, H), :], sib.at[it, c],
            sib_send.at[it, 0, c], sib_recv.at[it, 0, c], sibling,
        )

    def sib_ag(it, c, rows):
        part = pt.at[it + 1, c, pl.ds(rows, H), :]
        return remote(part, part, sib_send.at[it, 1, c], sib_recv.at[it, 1, c], sibling)

    def f_rs1(it, h, d):
        if h == 0:
            dest, dev = (x + d) % NX, xdev(d)
        else:
            dest, dev = (y + d) % NY, ydev(d)
        return remote(
            fp.at[it, pl.ds(2 * dest, 2), pl.ds(h * H, H), :], rx.at[it, h, d - 1],
            f_send.at[it, h, 0, d - 1], f_recv.at[it, h, 0, d - 1], dev,
        )

    def sub(h, k):
        return k // 2, pl.multiple_of((k % 2) * FR, FR)

    def f_rs2(it, h, d):
        if h == 0:
            dest, dev = (y + d) % NY, ydev(d)
        else:
            dest, dev = (x + d) % NX, xdev(d)
        b, s0 = sub(h, dest)
        return remote(
            g.at[it, h, b, pl.ds(s0, FR), :], ry.at[it, h, d - 1],
            f_send.at[it, h, 1, d - 1], f_recv.at[it, h, 1, d - 1], dev,
        )

    outer = (x, y)
    inner = (y, x)

    def f_ag1(it, h, d, k):
        b, s0 = sub(h, k)
        part = dt.at[it + 1, 2 * outer[h] + b, pl.ds(h * H + s0, FR), :]
        return remote(
            part, part, f_send.at[it, h, 2, d - 1], f_recv.at[it, h, 2, d - 1],
            ydev(d) if h == 0 else xdev(d),
        )

    def f_ag2(it, h, d, k):
        part = dt.at[it + 1, pl.ds(2 * k, 2), pl.ds(h * H, H), :]
        return remote(
            part, part, f_send.at[it, h, 3, d - 1], f_recv.at[it, h, 3, d - 1],
            xdev(d) if h == 0 else ydev(d),
        )

    far_first = (2, 1, 3)

    def iteration(it, _):
        for b in range(RB):
            dl[:, b * T : (b + 1) * T] = dt[it, b].astype(jnp.bfloat16)

        def adjoint_block(c):
            ap[it, c] = jnp.dot(dl[...], kd[c], preferred_element_type=jnp.float32)
            sib_rs(it, c).start()

        def dest_right(t):
            return (z + 9 - t) % NZ

        def dest_left(t):
            return (z + 8 + t) % NZ

        def adjoint_pair(t):
            adjoint_block(dest_right(t))
            adjoint_block(dest_left(t))

        def both(c, q):
            return (
                ap[it, c, pl.ds(own + q * HQ, HQ), :]
                + sib[it, c, pl.ds(q * HQ, HQ), :]
            )

        def rs_step(t, first, left):
            cr, cl = dest_right(t), dest_left(t)
            sib_rs(it, cr).wait_recv()
            if left:
                sib_rs(it, cl).wait_recv()
            for q in range(Q):
                value = both(cr, q)
                if not first:
                    rs_copy(it, 0, t - 1, q).wait_recv()
                    value = value + rs_r[it, 0, t - 2, q]
                rs_s[it, 0, t - 1, q] = value
                rs_copy(it, 0, t, q).start()
                if left:
                    value = both(cl, q)
                    if not first:
                        rs_copy(it, 1, t - 1, q).wait_recv()
                        value = value + rs_r[it, 1, t - 2, q]
                    rs_s[it, 1, t - 1, q] = value
                    rs_copy(it, 1, t, q).start()

        def primal_in(t):
            @pl.when(it == 0)
            def _():
                pt[0, 2 * (t - 1)] = primal0[2 * (t - 1)].T
                pt[0, 2 * (t - 1) + 1] = primal0[2 * (t - 1) + 1].T

        adjoint_pair(1)
        adjoint_pair(2)
        rs_step(1, True, True)
        adjoint_pair(3)
        primal_in(1)

        def rs_middle(t, _):
            rs_step(t, False, True)

            @pl.when(t <= 6)
            def _():
                adjoint_pair(t + 2)

            primal_in(t)
            return 0

        lax.fori_loop(2, 8, rs_middle, 0)
        rs_step(8, False, False)
        primal_in(8)

        sib_rs(it, z).wait_recv()
        cost_z = cost[pl.ds(z, 1), :]
        cap_z = cap[pl.ds(z, 1), :]
        for q in range(Q):
            rs_copy(it, 1, 7, q).wait_recv()
            part = both(z, q) + rs_r[it, 1, 6, q]
            rs_copy(it, 0, 8, q).wait_recv()
            adjoint = part + rs_r[it, 0, 7, q]
            rows = pl.ds(own + q * HQ, HQ)
            old = pt[it, z, rows, :]
            new = jnp.minimum(
                jnp.maximum(old - primal_step * (cost_z - adjoint), 0.0), cap_z
            )
            pt[it + 1, z, rows, :] = new
            ag_copy(it, 0, 1, q, z).start()
            ag_copy(it, 1, 1, q, z).start()
        sib_ag(it, z, own).start()

        def image(c):
            ext = (2.0 * pt[it + 1, c] - pt[it, c]).astype(jnp.bfloat16)
            return lax.dot_general(
                ext, kd[c], (((1,), (1,)), ((), ())), preferred_element_type=jnp.float32
            )

        def forward_one(c, first):
            sib_ag(it, c, oth).wait_recv()
            res = image(c)
            for b in range(RB):
                part = res[:, b * T : (b + 1) * T]
                fp[it, b] = part if first else fp[it, b] + part

        def forward_pair(t):
            cr, cl = (z - t + NZ) % NZ, (z + t) % NZ
            sib_ag(it, cr, oth).wait_recv()
            sib_ag(it, cl, oth).wait_recv()
            res = image(cr) + image(cl)
            for b in range(RB):
                fp[it, b] = fp[it, b] + res[:, b * T : (b + 1) * T]

        def ag_step(t, left, right_on, left_on):
            cr, cl = (z - t + NZ) % NZ, (z + t) % NZ
            for q in range(Q):
                ag_copy(it, 0, t, q, cr).wait_recv()
                if right_on:
                    ag_copy(it, 0, t + 1, q, cr).start()
                if left:
                    ag_copy(it, 1, t, q, cl).wait_recv()
                    if left_on:
                        ag_copy(it, 1, t + 1, q, cl).start()
            sib_ag(it, cr, own).start()
            if left:
                sib_ag(it, cl, own).start()

        ag_step(1, True, True, True)
        forward_one(z, True)

        def ag_middle(t, _):
            ag_step(t, True, True, True)
            forward_pair(t - 1)
            return 0

        lax.fori_loop(2, 7, ag_middle, 0)
        ag_step(7, True, True, False)
        forward_pair(6)
        ag_step(8, False, False, False)
        forward_pair(7)
        forward_one((z + 8) % NZ, False)

        for d in far_first:
            f_rs1(it, 0, d).start()
            f_rs1(it, 1, d).start()

        @pl.when(it == 0)
        def _():
            for h in range(2):
                b, _s = sub(h, inner[h])
                dem[h] = demand[2 * outer[h] + b].T

        @pl.when(it == ITERS - 1)
        def _():
            def leave(c, _):
                primal_out[c] = pt[ITERS, c].T
                return 0

            lax.fori_loop(0, CB, leave, 0)

        for h in range(2):
            for d in (1, 2, 3):
                f_rs1(it, h, d).wait_recv()
            rows = pl.ds(h * H, H)
            for b in range(2):
                g[it, h, b] = (
                    fp[it, 2 * outer[h] + b, rows, :]
                    + rx[it, h, 0, b]
                    + rx[it, h, 1, b]
                    + rx[it, h, 2, b]
                )
            for d in far_first:
                f_rs2(it, h, d).start()
        for h in range(2):
            for d in (1, 2, 3):
                f_rs2(it, h, d).wait_recv()
            b, s0 = sub(h, inner[h])
            forward = (
                g[it, h, b, pl.ds(s0, FR), :]
                + ry[it, h, 0]
                + ry[it, h, 1]
                + ry[it, h, 2]
            )
            block = 2 * outer[h] + b
            rows = pl.multiple_of(h * H + s0, FR)
            new = dt[it, block, pl.ds(rows, FR), :] + dual_step * (
                dem[h, pl.ds(rows, FR), :] - forward
            )
            new = jnp.where(
                kind[pl.ds(block, 1), :] == 1, jnp.maximum(new, 0.0), new
            )
            dt[it + 1, block, pl.ds(rows, FR), :] = new
            for d in far_first:
                f_ag1(it, h, d, inner[h]).start()
        for h in range(2):
            for d in (1, 2, 3):
                f_ag1(it, h, d, (inner[h] - d + 4) % 4).wait_recv()
            for d in far_first:
                f_ag2(it, h, d, outer[h]).start()
        for h in range(2):
            for d in (1, 2, 3):
                f_ag2(it, h, d, (outer[h] - d + 4) % 4).wait_recv()
        return 0

    lax.fori_loop(0, ITERS, iteration, 0)
    for b in range(RB):
        dual_out[b] = dt[ITERS, b].T

    def drain(it, _):
        def ring(t, _):
            for q in range(Q):
                rs_copy(it, 0, t, q).wait_send()
                ag_copy(it, 0, t, q, z).wait_send()

                @pl.when(t < 8)
                def _():
                    rs_copy(it, 1, t, q).wait_send()
                    ag_copy(it, 1, t, q, z).wait_send()

            return 0

        lax.fori_loop(1, 9, ring, 0)

        def blocks(c, _):
            sib_rs(it, c).wait_send()
            sib_ag(it, c, own).wait_send()
            return 0

        lax.fori_loop(0, CB, blocks, 0)
        for h in range(2):
            for d in (1, 2, 3):
                f_rs1(it, h, d).wait_send()
                f_rs2(it, h, d).wait_send()
                f_ag1(it, h, d, inner[h]).wait_send()
                f_ag2(it, h, d, outer[h]).wait_send()
        return 0

    lax.fori_loop(0, ITERS, drain, 0)


def per_device(
    tile_values,
    tile_row,
    tile_column,
    unit_cost,
    capacity,
    demand,
    row_kind,
    primal_start,
    dual_start,
):
    place = jnp.where(tile_row < RB, tile_row * CB + tile_column, RB * CB)
    slot = jnp.arange(SLOTS, dtype=jnp.int32)
    hit = place[:, None] == jnp.arange(RB * CB, dtype=jnp.int32)[None, :]
    inv = jnp.max(jnp.where(hit, slot[:, None], -1), axis=0)
    vmem = pl.BlockSpec(memory_space=pltpu.VMEM)
    f32, bf16 = jnp.float32, jnp.bfloat16
    dma = pltpu.SemaphoreType.DMA
    return pl.pallas_call(
        kernel,
        out_shape=(
            jax.ShapeDtypeStruct((CB, T, S), f32),
            jax.ShapeDtypeStruct((RB, T, S), f32),
        ),
        in_specs=[pl.BlockSpec(memory_space=pltpu.SMEM)] + [vmem] * 7,
        out_specs=(vmem, vmem),
        scratch_shapes=[
            pltpu.VMEM((CB, RB * T, T), bf16),
            pltpu.VMEM((ITERS + 1, CB, S, T), f32),
            pltpu.VMEM((ITERS + 1, RB, S, T), f32),
            pltpu.VMEM((S, RB * T), bf16),
            pltpu.VMEM((ITERS, CB, S, T), f32),
            pltpu.VMEM((ITERS, CB, H, T), f32),
            pltpu.VMEM((ITERS, 2, 8, Q, HQ, T), f32),
            pltpu.VMEM((ITERS, 2, 8, Q, HQ, T), f32),
            pltpu.VMEM((ITERS, RB, S, T), f32),
            pltpu.VMEM((ITERS, 2, 3, 2, H, T), f32),
            pltpu.VMEM((ITERS, 2, 2, H, T), f32),
            pltpu.VMEM((ITERS, 2, 3, FR, T), f32),
            pltpu.VMEM((2, S, T), f32),
            dma((ITERS, 2, 2, 8, Q)),
            dma((ITERS, 2, 2, 8, Q)),
            dma((ITERS, 2, CB)),
            dma((ITERS, 2, CB)),
            dma((ITERS, 2, 4, 3)),
            dma((ITERS, 2, 4, 3)),
        ],
        compiler_params=pltpu.CompilerParams(
            collective_id=0, has_side_effects=True, vmem_limit_bytes=48 << 20
        ),
        cost_estimate=pl.CostEstimate(
            flops=8 * SLOTS * T * T * S, bytes_accessed=6 << 20, transcendentals=0
        ),
    )(
        inv,
        tile_values,
        unit_cost,
        capacity,
        demand,
        row_kind,
        primal_start,
        dual_start,
    )


def solution(mesh):
    placed = (
        P(("col", "row"), None, None),
        P(("col", "row")),
        P(("col", "row")),
        P("col", None),
        P("col", None),
        P("row", None, None),
        P("row", None),
        P("col", None, None),
        P("row", None, None),
    )
    return jax.shard_map(
        per_device,
        mesh=mesh,
        in_specs=placed,
        out_specs=(P("col", None, None), P("row", None, None)),
        check_vma=False,
    )
```

```python
import jax
import jax.numpy as jnp
from jax import lax
from jax.experimental import pallas as pl
from jax.experimental.pallas import tpu as pltpu
from jax.sharding import PartitionSpec as P

ITERS = 2
NX, NY, NZ = 4, 4, 16
RB, CB, T, S = 8, 16, 128, 128
H = S // 2
FR = 32
SLOTS = 48

PARENT = {1: 0, 4: 0, 2: 1, 5: 4, 7: 4, 3: 2, 6: 5, 8: 7}
LEVELS = ((0,), (4, 1), (7, 5, 2), (8, 6, 3))
OFFS = (0, 1, -1, 4, -4, 2, -2, 5, -5, 7, -7, 3, -3, 6, -6, 8)
POS = {o: p for p, o in enumerate(OFFS)}
POS[-8] = POS[8]
GROUPS = ((0, 1), (1, 5), (5, 11), (11, 16))
HOPS = sorted({s * (d - u) for d, u in PARENT.items() for s in (1, -1)})

primal_step = 0.5
dual_step = 0.5


def children(d):
    return [c for c, u in PARENT.items() if u == d]


def half(s, d):
    if d == 8:
        return (0 if s == 1 else H // 2), H // 2
    return 0, H


def kernel(
    inv_ref,
    tiles_hbm,
    cost_hbm,
    cap_hbm,
    demand_hbm,
    kind_hbm,
    primal_hbm,
    dual_hbm,
    primal_out,
    dual_out,
    tiles,
    cost,
    cap,
    kind,
    primal0,
    dual0,
    dem0,
    kd,
    pt,
    dt,
    dl,
    ext,
    ap,
    sib,
    rs_s,
    rs_r,
    fp,
    rx,
    g,
    ry,
    dem,
    local_sem,
    ring_send,
    ring_recv,
    sib_send,
    sib_recv,
    f_send,
    f_recv,
):
    col = lax.axis_index("col")
    row = lax.axis_index("row")
    x, y = col // NY, col % NY
    z, core = row // 2, row % 2
    own = pl.multiple_of(core * H, H)
    oth = pl.multiple_of((1 - core) * H, H)
    outer = (x, y)
    inner = (y, x)

    def block_at(p):
        return (z + OFFS[p] + NZ) % NZ

    def zdev(d):
        return (col, ((z + d + NZ) % NZ) * 2 + core)

    sibling = (col, z * 2 + 1 - core)

    def xdev(d):
        return (((x + d) % NX) * NY + y, row)

    def ydev(d):
        return (x * NY + (y + d) % NY, row)

    def sub(h, k):
        return k // 2, pl.multiple_of((k % 2) * FR, FR)

    dem_block = [2 * outer[h] + sub(h, inner[h])[0] for h in range(2)]
    loads = [
        pltpu.make_async_copy(src, dst, local_sem.at[n])
        for n, (src, dst) in enumerate(
            [
                (dual_hbm, dual0),
                (tiles_hbm, tiles),
                (primal_hbm, primal0),
                (cost_hbm, cost),
                (cap_hbm, cap),
                (kind_hbm, kind),
                (demand_hbm.at[dem_block[0]], dem0.at[0]),
                (demand_hbm.at[dem_block[1]], dem0.at[1]),
            ]
        )
    ]
    for load in loads:
        load.start()

    barrier = pltpu.get_barrier_semaphore()
    peers = [zdev(d) for d in HOPS] + [sibling]
    peers += [xdev(d) for d in (1, 2, 3)] + [ydev(d) for d in (1, 2, 3)]
    for peer in peers:
        pl.semaphore_signal(
            barrier, inc=1, device_id=peer, device_id_type=pl.DeviceIdType.MESH
        )

    def remote(src, dst, ss, rs, dev):
        return pltpu.make_async_remote_copy(
            src_ref=src,
            dst_ref=dst,
            send_sem=ss,
            recv_sem=rs,
            device_id=dev,
            device_id_type=pl.DeviceIdType.MESH,
        )

    def side(s):
        return 0 if s == 1 else 1

    def rs_copy(it, s, d):
        i = (it, side(s), d - 1, pl.ds(0, half(s, d)[1]))
        return remote(
            rs_s.at[i], rs_r.at[i], ring_send.at[it, 0, side(s), d - 1],
            ring_recv.at[it, 0, side(s), d - 1], zdev(s * (d - PARENT[d])),
        )

    def ag_part(it, p, s, d):
        start, size = half(s, d)
        return pt.at[it + 1, p, pl.ds(pl.multiple_of(own + start, 32), size), :]

    def ag_copy(it, s, d):
        return remote(
            ag_part(it, POS[-s * PARENT[d]], s, d), ag_part(it, POS[-s * d], s, d),
            ring_send.at[it, 1, side(s), d - 1],
            ring_recv.at[it, 1, side(s), d - 1], zdev(s * (d - PARENT[d])),
        )

    def sib_rs(it, lo, hi):
        return remote(
            ap.at[it, lo:hi, pl.ds(oth, H), :], sib.at[it, lo:hi],
            sib_send.at[it, 0, lo], sib_recv.at[it, 0, lo], sibling,
        )

    def sib_ag(it, n, rows):
        lo, hi = GROUPS[n]
        part = pt.at[it + 1, lo:hi, pl.ds(rows, H), :]
        return remote(part, part, sib_send.at[it, 1, lo], sib_recv.at[it, 1, lo], sibling)

    def f_rs1(it, h, d):
        if h == 0:
            dest, dev = (x + d) % NX, xdev(d)
        else:
            dest, dev = (y + d) % NY, ydev(d)
        return remote(
            fp.at[it, pl.ds(2 * dest, 2), pl.ds(h * H, H), :], rx.at[it, h, d - 1],
            f_send.at[it, h, 0, d - 1], f_recv.at[it, h, 0, d - 1], dev,
        )

    def f_rs2(it, h, d):
        if h == 0:
            dest, dev = (y + d) % NY, ydev(d)
        else:
            dest, dev = (x + d) % NX, xdev(d)
        b, s0 = sub(h, dest)
        return remote(
            g.at[it, h, b, pl.ds(s0, FR), :], ry.at[it, h, d - 1],
            f_send.at[it, h, 1, d - 1], f_recv.at[it, h, 1, d - 1], dev,
        )

    def f_ag1(it, h, d, k):
        b, s0 = sub(h, k)
        part = dt.at[it + 1, 2 * outer[h] + b, pl.ds(h * H + s0, FR), :]
        return remote(
            part, part, f_send.at[it, h, 2, d - 1], f_recv.at[it, h, 2, d - 1],
            ydev(d) if h == 0 else xdev(d),
        )

    def f_ag2(it, h, d, k):
        part = dt.at[it + 1, pl.ds(2 * k, 2), pl.ds(h * H, H), :]
        return remote(
            part, part, f_send.at[it, h, 3, d - 1], f_recv.at[it, h, 3, d - 1],
            xdev(d) if h == 0 else ydev(d),
        )

    far_first = (2, 1, 3)

    def build(lo, hi):
        def rows_of(r, _):
            r0 = pl.multiple_of(r * T, T)
            for p in range(lo, hi):
                idx = inv_ref[r * CB + block_at(p)]
                tile = tiles[jnp.maximum(idx, 0)].astype(jnp.float32)
                tile = jnp.where(idx >= 0, tile, 0.0).astype(jnp.bfloat16)
                kd[pl.ds(r0, T), p * T : (p + 1) * T] = tile
            return 0

        lax.fori_loop(0, RB, rows_of, 0)

    def iteration(it, _):
        def adjoint(lo, hi):
            @pl.when(it == 0)
            def _():
                build(lo, hi)

            for p in range(lo, hi, 2):
                n = min(2, hi - p)
                res = jnp.dot(
                    dl[...],
                    kd[:, p * T : (p + n) * T],
                    preferred_element_type=jnp.float32,
                )
                for k in range(n):
                    ap[it, p + k] = res[:, k * T : (k + 1) * T]
            sib_rs(it, lo, hi).start()

        def rs_node(s, d):
            p = POS[s * d]
            start, size = half(s, d)
            value = (
                ap[it, p, pl.ds(pl.multiple_of(own + start, 32), size), :]
                + sib[it, p, start : start + size, :]
            )
            full = []
            for c in children(d):
                rs_copy(it, s, c).wait_recv()
                if c != 8:
                    value = value + rs_r[it, side(s), c - 1]
                else:
                    full.append(c)
            rs_s[it, side(s), d - 1, :size] = value
            for c in full:
                at, many = half(s, c)
                rows = slice(at, at + many)
                rs_s[it, side(s), d - 1, rows] = (
                    rs_s[it, side(s), d - 1, rows] + rs_r[it, side(s), c - 1, :many]
                )
            rs_copy(it, s, d).start()

        @pl.when(it == 0)
        def _():
            loads[0].wait()
            for b in range(RB):
                dt[0, b] = dual0[b].T
            loads[1].wait()

        for b in range(RB):
            dl[:, b * T : (b + 1) * T] = dt[it, b].astype(jnp.bfloat16)

        @pl.when(it == 0)
        def _():
            pl.semaphore_wait(barrier, len(peers))

        adjoint(11, 16)
        adjoint(5, 11)
        sib_rs(it, 11, 16).wait_recv()
        for d in LEVELS[3]:
            for s in (1, -1):
                rs_node(s, d)
        adjoint(0, 5)
        sib_rs(it, 5, 11).wait_recv()
        for d in LEVELS[2]:
            for s in (1, -1):
                rs_node(s, d)

        @pl.when(it == 0)
        def _():
            for load in loads[2:]:
                load.wait()
            for p in range(CB):
                pt[0, p] = primal0[block_at(p)].T
            for h in range(2):
                dem[h] = dem0[h].T

        sib_rs(it, 0, 5).wait_recv()
        for d in LEVELS[1]:
            for s in (1, -1):
                rs_node(s, d)

        total = ap[it, 0, pl.ds(own, H), :] + sib[it, 0]
        for d in reversed(LEVELS[1]):
            for s in (1, -1):
                rs_copy(it, s, d).wait_recv()
                total = total + rs_r[it, side(s), d - 1]
        old = pt[it, 0, pl.ds(own, H), :]
        pt[it + 1, 0, pl.ds(own, H), :] = jnp.minimum(
            jnp.maximum(old - primal_step * (cost[pl.ds(z, 1), :] - total), 0.0),
            cap[pl.ds(z, 1), :],
        )
        for d in LEVELS[1]:
            for s in (1, -1):
                ag_copy(it, s, d).start()
        sib_ag(it, 0, own).start()

        def ag_level(n, order):
            for d in order:
                for s in (1, -1):
                    ag_copy(it, s, d).wait_recv()
                    for c in reversed(children(d)):
                        ag_copy(it, s, c).start()
            sib_ag(it, n, own).start()

        def forward(lo, hi, first):
            for p in range(lo, hi):
                ext[:, p * T : (p + 1) * T] = (
                    2.0 * pt[it + 1, p] - pt[it, p]
                ).astype(jnp.bfloat16)
            for n in range(0, RB, 2):
                res = lax.dot_general(
                    ext[:, lo * T : hi * T],
                    kd[n * T : (n + 2) * T, lo * T : hi * T],
                    (((1,), (1,)), ((), ())),
                    preferred_element_type=jnp.float32,
                )
                for k in range(2):
                    part = res[:, k * T : (k + 1) * T]
                    fp[it, n + k] = part if first else fp[it, n + k] + part

        ag_level(1, (1, 4))
        ag_level(2, (2, 5, 7))
        sib_ag(it, 0, oth).wait_recv()
        sib_ag(it, 1, oth).wait_recv()
        forward(0, 5, True)
        ag_level(3, (3, 6, 8))
        sib_ag(it, 2, oth).wait_recv()
        forward(5, 11, False)
        sib_ag(it, 3, oth).wait_recv()
        forward(11, 16, False)

        for d in far_first:
            f_rs1(it, 0, d).start()
            f_rs1(it, 1, d).start()

        @pl.when(it == ITERS - 1)
        def _():
            for p in range(CB):
                primal_out[block_at(p)] = pt[ITERS, p].T

        for h in range(2):
            for d in (1, 2, 3):
                f_rs1(it, h, d).wait_recv()
            rows = pl.ds(h * H, H)
            for b in range(2):
                g[it, h, b] = (
                    fp[it, 2 * outer[h] + b, rows, :]
                    + rx[it, h, 0, b]
                    + rx[it, h, 1, b]
                    + rx[it, h, 2, b]
                )
            for d in far_first:
                f_rs2(it, h, d).start()
        for h in range(2):
            for d in (1, 2, 3):
                f_rs2(it, h, d).wait_recv()
            b, s0 = sub(h, inner[h])
            forward = (
                g[it, h, b, pl.ds(s0, FR), :]
                + ry[it, h, 0]
                + ry[it, h, 1]
                + ry[it, h, 2]
            )
            block = 2 * outer[h] + b
            rows = pl.multiple_of(h * H + s0, FR)
            new = dt[it, block, pl.ds(rows, FR), :] + dual_step * (
                dem[h, pl.ds(rows, FR), :] - forward
            )
            new = jnp.where(
                kind[pl.ds(block, 1), :] == 1, jnp.maximum(new, 0.0), new
            )
            dt[it + 1, block, pl.ds(rows, FR), :] = new
            for d in far_first:
                f_ag1(it, h, d, inner[h]).start()
        for h in range(2):
            for d in (1, 2, 3):
                f_ag1(it, h, d, (inner[h] - d + 4) % 4).wait_recv()
            for d in far_first:
                f_ag2(it, h, d, outer[h]).start()
        for h in range(2):
            for d in (1, 2, 3):
                f_ag2(it, h, d, (outer[h] - d + 4) % 4).wait_recv()
        return 0

    lax.fori_loop(0, ITERS, iteration, 0)
    for b in range(RB):
        dual_out[b] = dt[ITERS, b].T

    def drain(it, _):
        for s in (1, -1):
            for d in PARENT:
                rs_copy(it, s, d).wait_send()
                ag_copy(it, s, d).wait_send()
        for n in range(4):
            sib_ag(it, n, own).wait_send()
        for lo, hi in ((0, 5), (5, 11), (11, 16)):
            sib_rs(it, lo, hi).wait_send()
        for h in range(2):
            for d in (1, 2, 3):
                f_rs1(it, h, d).wait_send()
                f_rs2(it, h, d).wait_send()
                f_ag1(it, h, d, inner[h]).wait_send()
                f_ag2(it, h, d, outer[h]).wait_send()
        return 0

    lax.fori_loop(0, ITERS, drain, 0)


def per_device(
    tile_values,
    tile_row,
    tile_column,
    unit_cost,
    capacity,
    demand,
    row_kind,
    primal_start,
    dual_start,
):
    place = jnp.where(tile_row < RB, tile_row * CB + tile_column, RB * CB)
    slot = jnp.arange(SLOTS, dtype=jnp.int32)
    hit = place[:, None] == jnp.arange(RB * CB, dtype=jnp.int32)[None, :]
    inv = jnp.max(jnp.where(hit, slot[:, None], -1), axis=0)
    vmem = pl.BlockSpec(memory_space=pltpu.VMEM)
    f32, bf16 = jnp.float32, jnp.bfloat16
    dma = pltpu.SemaphoreType.DMA
    return pl.pallas_call(
        kernel,
        out_shape=(
            jax.ShapeDtypeStruct((CB, T, S), f32),
            jax.ShapeDtypeStruct((RB, T, S), f32),
        ),
        in_specs=[pl.BlockSpec(memory_space=pltpu.SMEM)]
        + [pl.BlockSpec(memory_space=pl.ANY)] * 7,
        out_specs=(vmem, vmem),
        scratch_shapes=[
            pltpu.VMEM((SLOTS, T, T), bf16),
            pltpu.VMEM((CB, T), f32),
            pltpu.VMEM((CB, T), f32),
            pltpu.VMEM((RB, T), jnp.int32),
            pltpu.VMEM((CB, T, S), f32),
            pltpu.VMEM((RB, T, S), f32),
            pltpu.VMEM((2, T, S), f32),
            pltpu.VMEM((RB * T, CB * T), bf16),
            pltpu.VMEM((ITERS + 1, CB, S, T), f32),
            pltpu.VMEM((ITERS + 1, RB, S, T), f32),
            pltpu.VMEM((S, RB * T), bf16),
            pltpu.VMEM((S, CB * T), bf16),
            pltpu.VMEM((ITERS, CB, S, T), f32),
            pltpu.VMEM((ITERS, CB, H, T), f32),
            pltpu.VMEM((ITERS, 2, 8, H, T), f32),
            pltpu.VMEM((ITERS, 2, 8, H, T), f32),
            pltpu.VMEM((ITERS, RB, S, T), f32),
            pltpu.VMEM((ITERS, 2, 3, 2, H, T), f32),
            pltpu.VMEM((ITERS, 2, 2, H, T), f32),
            pltpu.VMEM((ITERS, 2, 3, FR, T), f32),
            pltpu.VMEM((2, S, T), f32),
            dma((8,)),
            dma((ITERS, 2, 2, 8)),
            dma((ITERS, 2, 2, 8)),
            dma((ITERS, 2, CB)),
            dma((ITERS, 2, CB)),
            dma((ITERS, 2, 4, 3)),
            dma((ITERS, 2, 4, 3)),
        ],
        compiler_params=pltpu.CompilerParams(
            collective_id=0, has_side_effects=True, vmem_limit_bytes=56 << 20
        ),
        cost_estimate=pl.CostEstimate(
            flops=8 * SLOTS * T * T * S, bytes_accessed=6 << 20, transcendentals=0
        ),
    )(
        inv,
        tile_values,
        unit_cost,
        capacity,
        demand,
        row_kind,
        primal_start,
        dual_start,
    )


def solution(mesh):
    placed = (
        P(("col", "row"), None, None),
        P(("col", "row")),
        P(("col", "row")),
        P("col", None),
        P("col", None),
        P("row", None, None),
        P("row", None),
        P("col", None, None),
        P("row", None, None),
    )
    return jax.shard_map(
        per_device,
        mesh=mesh,
        in_specs=placed,
        out_specs=(P("col", None, None), P("row", None, None)),
        check_vma=False,
    )
```

```python
import jax
import jax.numpy as jnp
from jax import lax
from jax.experimental import pallas as pl
from jax.experimental.pallas import tpu as pltpu
from jax.sharding import PartitionSpec as P

ITERS = 2
NX, NY, NZ = 4, 4, 16
RB, CB, T, S = 8, 16, 128, 128
NQ = 2
SQ = S // NQ
H = SQ // 2
FR = H // 2
SLOTS = 48

PARENT = {1: 0, 4: 0, 2: 1, 5: 4, 7: 4, 3: 2, 6: 5, 8: 7}
LEVELS = ((0,), (4, 1), (7, 5, 2), (8, 6, 3))
OFFS = (0, 1, -1, 4, -4, 2, -2, 5, -5, 7, -7, 3, -3, 6, -6, 8)
POS = {o: p for p, o in enumerate(OFFS)}
POS[-8] = POS[8]
PARTS = ((0, 5), (5, 11), (11, 16))
GROUPS = ((0, 1), (1, 5), (5, 11), (11, 16))
HOPS = sorted({s * (d - u) for d, u in PARENT.items() for s in (1, -1)})

primal_step = 0.5
dual_step = 0.5


def children(d):
    return [c for c, u in PARENT.items() if u == d]


def half(s, d):
    if d == 8:
        return (0 if s == 1 else H // 2), H // 2
    return 0, H


def kernel(
    inv_ref,
    tiles_hbm,
    cost_hbm,
    cap_hbm,
    demand_hbm,
    kind_hbm,
    primal_hbm,
    dual_hbm,
    primal_out,
    dual_out,
    tiles,
    cost,
    cap,
    kind,
    primal0,
    dual0,
    dem0,
    kd,
    pt,
    dt,
    dl,
    ext,
    ap,
    sib,
    rs_s,
    rs_r,
    fp,
    rx,
    g,
    ry,
    dem,
    local_sem,
    ring_send,
    ring_recv,
    sib_send,
    sib_recv,
    f_send,
    f_recv,
):
    col = lax.axis_index("col")
    row = lax.axis_index("row")
    x, y = col // NY, col % NY
    z, core = row // 2, row % 2

    def own(q):
        return pl.multiple_of(q * SQ + core * H, H)

    def oth(q):
        return pl.multiple_of(q * SQ + (1 - core) * H, H)

    outer = (x, y)
    inner = (y, x)

    def block_at(p):
        return (z + OFFS[p] + NZ) % NZ

    def zdev(d):
        return (col, ((z + d + NZ) % NZ) * 2 + core)

    sibling = (col, z * 2 + 1 - core)

    def xdev(d):
        return (((x + d) % NX) * NY + y, row)

    def ydev(d):
        return (x * NY + (y + d) % NY, row)

    def sub(k):
        return k // 2, pl.multiple_of((k % 2) * FR, FR)

    dem_block = [2 * outer[h] + sub(inner[h])[0] for h in range(2)]
    loads = [
        pltpu.make_async_copy(src, dst, local_sem.at[n])
        for n, (src, dst) in enumerate(
            [
                (dual_hbm, dual0),
                (tiles_hbm, tiles),
                (primal_hbm, primal0),
                (cost_hbm, cost),
                (cap_hbm, cap),
                (kind_hbm, kind),
                (demand_hbm.at[dem_block[0]], dem0.at[0]),
                (demand_hbm.at[dem_block[1]], dem0.at[1]),
            ]
        )
    ]
    for load in loads:
        load.start()

    barrier = pltpu.get_barrier_semaphore()
    peers = [zdev(d) for d in HOPS] + [sibling]
    peers += [xdev(d) for d in (1, 2, 3)] + [ydev(d) for d in (1, 2, 3)]
    for peer in peers:
        pl.semaphore_signal(
            barrier, inc=1, device_id=peer, device_id_type=pl.DeviceIdType.MESH
        )

    def remote(src, dst, ss, rs, dev):
        return pltpu.make_async_remote_copy(
            src_ref=src,
            dst_ref=dst,
            send_sem=ss,
            recv_sem=rs,
            device_id=dev,
            device_id_type=pl.DeviceIdType.MESH,
        )

    def side(s):
        return 0 if s == 1 else 1

    def rs_copy(it, q, s, d):
        i = (it, q, side(s), d - 1, pl.ds(0, half(s, d)[1]))
        return remote(
            rs_s.at[i], rs_r.at[i], ring_send.at[it, 0, q, side(s), d - 1],
            ring_recv.at[it, 0, q, side(s), d - 1], zdev(s * (d - PARENT[d])),
        )

    def own_rows(q, s, d):
        start, size = half(s, d)
        return pl.ds(pl.multiple_of(own(q) + start, 16), size)

    def ag_copy(it, q, s, d):
        rows = own_rows(q, s, d)
        return remote(
            pt.at[it + 1, POS[-s * PARENT[d]], rows, :],
            pt.at[it + 1, POS[-s * d], rows, :],
            ring_send.at[it, 1, q, side(s), d - 1],
            ring_recv.at[it, 1, q, side(s), d - 1], zdev(s * (d - PARENT[d])),
        )

    def sib_rs(it, q, n):
        lo, hi = PARTS[n]
        return remote(
            ap.at[it, lo:hi, pl.ds(oth(q), H), :], sib.at[it, q, lo:hi],
            sib_send.at[it, 0, q, n], sib_recv.at[it, 0, q, n], sibling,
        )

    def sib_ag(it, q, n, rows):
        lo, hi = GROUPS[n]
        part = pt.at[it + 1, lo:hi, pl.ds(rows, H), :]
        return remote(
            part, part, sib_send.at[it, 1, q, n], sib_recv.at[it, 1, q, n], sibling
        )

    def f_dev(h, d, first):
        return xdev(d) if (h == 0) == first else ydev(d)

    def f_sem(it, q, h, phase, d):
        i = (it, q, h, phase, d - 1)
        return f_send.at[i], f_recv.at[i]

    def f_rs1(it, q, h, d):
        dest = (outer[h] + d) % 4
        return remote(
            fp.at[it, pl.ds(2 * dest, 2), pl.ds(q * SQ + h * H, H), :],
            rx.at[it, q, h, d - 1], *f_sem(it, q, h, 0, d), f_dev(h, d, True),
        )

    def f_rs2(it, q, h, d):
        b, s0 = sub((inner[h] + d) % 4)
        return remote(
            g.at[it, q, h, b, pl.ds(s0, FR), :], ry.at[it, q, h, d - 1],
            *f_sem(it, q, h, 1, d), f_dev(h, d, False),
        )

    def f_rows(q, h, s0):
        return pl.ds(pl.multiple_of(q * SQ + h * H + s0, FR), FR)

    def f_ag1(it, q, h, d, k):
        b, s0 = sub(k)
        part = dt.at[it + 1, 2 * outer[h] + b, f_rows(q, h, s0), :]
        return remote(part, part, *f_sem(it, q, h, 2, d), f_dev(h, d, False))

    def f_ag2(it, q, h, d, k):
        part = dt.at[it + 1, pl.ds(2 * k, 2), pl.ds(q * SQ + h * H, H), :]
        return remote(part, part, *f_sem(it, q, h, 3, d), f_dev(h, d, True))

    far_first = (2, 1, 3)

    def build(lo, hi):
        def rows_of(r, _):
            r0 = pl.multiple_of(r * T, T)
            for p in range(lo, hi):
                idx = inv_ref[r * CB + block_at(p)]
                tile = tiles[jnp.maximum(idx, 0)]
                tile = jnp.where(idx >= 0, tile, jnp.zeros_like(tile))
                kd[pl.ds(r0, T), p * T : (p + 1) * T] = tile
            return 0

        lax.fori_loop(0, RB, rows_of, 0)

    def f_ag2_wait(it, q):
        for h in range(2):
            for d in (1, 2, 3):
                f_ag2(it, q, h, d, (outer[h] - d + 4) % 4).wait_recv()

    both = (0, S)

    def slab(q):
        return (q * SQ, SQ)

    def iteration(it, _):
        def adjoint(n, rows):
            lo, hi = PARTS[n]
            r0, many = rows
            for p in range(lo, hi, 2):
                w = min(2, hi - p)
                res = jnp.dot(
                    dl[r0 : r0 + many, :],
                    kd[:, p * T : (p + w) * T],
                    preferred_element_type=jnp.float32,
                )
                for k in range(w):
                    ap[it, p + k, r0 : r0 + many] = res[:, k * T : (k + 1) * T]

        def build_first(n):
            @pl.when(it == 0)
            def _():
                build(*PARTS[n])

        def rs_node(q, s, d):
            p = POS[s * d]
            start, size = half(s, d)
            value = (
                ap[it, p, own_rows(q, s, d), :] + sib[it, q, p, start : start + size, :]
            )
            for c in children(d):
                rs_copy(it, q, s, c).wait_recv()
                if c != 8:
                    value = value + rs_r[it, q, side(s), c - 1]
            rs_s[it, q, side(s), d - 1, :size] = value
            if 8 in children(d):
                at, many = half(s, 8)
                rows = slice(at, at + many)
                rs_s[it, q, side(s), d - 1, rows] = (
                    rs_s[it, q, side(s), d - 1, rows] + rs_r[it, q, side(s), 7, :many]
                )
            rs_copy(it, q, s, d).start()

        def rs_level(n):
            for q in range(NQ):
                sib_rs(it, q, n - 1).wait_recv()
                for d in LEVELS[n]:
                    for s in (1, -1):
                        rs_node(q, s, d)

        @pl.when(it == 0)
        def _():
            loads[0].wait()
            for b in range(RB):
                dt[0, b] = dual0[b].T
            loads[1].wait()
            build(*PARTS[2])
            pl.semaphore_wait(barrier, len(peers))

        for q in range(NQ):

            @pl.when(it > 0)
            def _():
                f_ag2_wait(it - 1, q)

            r0, many = slab(q)
            for b in range(RB):
                dl[r0 : r0 + many, b * T : (b + 1) * T] = dt[
                    it, b, r0 : r0 + many
                ].astype(jnp.bfloat16)
            adjoint(2, slab(q))
            sib_rs(it, q, 2).start()

        build_first(1)
        adjoint(1, both)
        for q in range(NQ):
            sib_rs(it, q, 1).start()
        rs_level(3)
        build_first(0)
        adjoint(0, both)
        for q in range(NQ):
            sib_rs(it, q, 0).start()
        rs_level(2)

        @pl.when(it == 0)
        def _():
            for load in loads[2:]:
                load.wait()
            for p in range(CB):
                pt[0, p] = primal0[block_at(p)].T
            for h in range(2):
                dem[h] = dem0[h].T

        rs_level(1)

        for q in range(NQ):
            rows = pl.ds(own(q), H)
            total = ap[it, 0, rows, :] + sib[it, q, 0]
            for d in reversed(LEVELS[1]):
                for s in (1, -1):
                    rs_copy(it, q, s, d).wait_recv()
                    total = total + rs_r[it, q, side(s), d - 1]
            old = pt[it, 0, rows, :]
            pt[it + 1, 0, rows, :] = jnp.minimum(
                jnp.maximum(old - primal_step * (cost[pl.ds(z, 1), :] - total), 0.0),
                cap[pl.ds(z, 1), :],
            )
            for d in LEVELS[1]:
                for s in (1, -1):
                    ag_copy(it, q, s, d).start()
            sib_ag(it, q, 0, own(q)).start()

        def ag_level(n):
            for q in range(NQ):
                for d in reversed(LEVELS[n]):
                    for s in (1, -1):
                        ag_copy(it, q, s, d).wait_recv()
                        for c in reversed(children(d)):
                            ag_copy(it, q, s, c).start()
                sib_ag(it, q, n, own(q)).start()

        def forward(lo, hi, rows, first):
            r0, many = rows
            at = slice(r0, r0 + many)
            for p in range(lo, hi):
                ext[at, p * T : (p + 1) * T] = (
                    2.0 * pt[it + 1, p, at] - pt[it, p, at]
                ).astype(jnp.bfloat16)
            for n in range(0, RB, 2):
                res = lax.dot_general(
                    ext[at, lo * T : hi * T],
                    kd[n * T : (n + 2) * T, lo * T : hi * T],
                    (((1,), (1,)), ((), ())),
                    preferred_element_type=jnp.float32,
                )
                for k in range(2):
                    part = res[:, k * T : (k + 1) * T]
                    fp[it, n + k, at] = part if first else fp[it, n + k, at] + part

        ag_level(1)
        ag_level(2)
        for q in range(NQ):
            sib_ag(it, q, 0, oth(q)).wait_recv()
            sib_ag(it, q, 1, oth(q)).wait_recv()
        forward(0, 5, both, True)
        ag_level(3)
        for q in range(NQ):
            sib_ag(it, q, 2, oth(q)).wait_recv()
        forward(5, 11, both, False)

        for q in range(NQ):
            sib_ag(it, q, 3, oth(q)).wait_recv()
            forward(11, 16, slab(q), False)
            for d in far_first:
                for h in range(2):
                    f_rs1(it, q, h, d).start()

        @pl.when(it == ITERS - 1)
        def _():
            for p in range(CB):
                primal_out[block_at(p)] = pt[ITERS, p].T

        for q in range(NQ):
            for h in range(2):
                for d in (1, 3, 2):
                    f_rs1(it, q, h, d).wait_recv()
                for b in range(2):
                    g[it, q, h, b] = (
                        fp[it, 2 * outer[h] + b, q * SQ + h * H : q * SQ + (h + 1) * H]
                        + rx[it, q, h, 0, b]
                        + rx[it, q, h, 1, b]
                        + rx[it, q, h, 2, b]
                    )
                for d in far_first:
                    f_rs2(it, q, h, d).start()
        for q in range(NQ):
            for h in range(2):
                for d in (1, 3, 2):
                    f_rs2(it, q, h, d).wait_recv()
                b, s0 = sub(inner[h])
                forward_sum = (
                    g[it, q, h, b, pl.ds(s0, FR), :]
                    + ry[it, q, h, 0]
                    + ry[it, q, h, 1]
                    + ry[it, q, h, 2]
                )
                block = 2 * outer[h] + b
                rows = f_rows(q, h, s0)
                new = dt[it, block, rows, :] + dual_step * (
                    dem[h, rows, :] - forward_sum
                )
                new = jnp.where(
                    kind[pl.ds(block, 1), :] == 1, jnp.maximum(new, 0.0), new
                )
                dt[it + 1, block, rows, :] = new
                for d in far_first:
                    f_ag1(it, q, h, d, inner[h]).start()
        for q in range(NQ):
            for h in range(2):
                for d in (1, 3, 2):
                    f_ag1(it, q, h, d, (inner[h] - d + 4) % 4).wait_recv()
                for d in far_first:
                    f_ag2(it, q, h, d, outer[h]).start()
        return 0

    lax.fori_loop(0, ITERS, iteration, 0)
    for q in range(NQ):
        f_ag2_wait(ITERS - 1, q)
    for b in range(RB):
        dual_out[b] = dt[ITERS, b].T

    def drain(it, _):
        for q in range(NQ):
            for s in (1, -1):
                for d in PARENT:
                    rs_copy(it, q, s, d).wait_send()
                    ag_copy(it, q, s, d).wait_send()
            for n in range(len(GROUPS)):
                sib_ag(it, q, n, own(q)).wait_send()
            for n in range(len(PARTS)):
                sib_rs(it, q, n).wait_send()
            for h in range(2):
                for d in (1, 2, 3):
                    f_rs1(it, q, h, d).wait_send()
                    f_rs2(it, q, h, d).wait_send()
                    f_ag1(it, q, h, d, inner[h]).wait_send()
                    f_ag2(it, q, h, d, outer[h]).wait_send()
        return 0

    lax.fori_loop(0, ITERS, drain, 0)


def per_device(
    tile_values,
    tile_row,
    tile_column,
    unit_cost,
    capacity,
    demand,
    row_kind,
    primal_start,
    dual_start,
):
    place = jnp.where(tile_row < RB, tile_row * CB + tile_column, RB * CB)
    slot = jnp.arange(SLOTS, dtype=jnp.int32)
    hit = place[:, None] == jnp.arange(RB * CB, dtype=jnp.int32)[None, :]
    inv = jnp.max(jnp.where(hit, slot[:, None], -1), axis=0)
    vmem = pl.BlockSpec(memory_space=pltpu.VMEM)
    f32, bf16 = jnp.float32, jnp.bfloat16
    dma = pltpu.SemaphoreType.DMA
    return pl.pallas_call(
        kernel,
        out_shape=(
            jax.ShapeDtypeStruct((CB, T, S), f32),
            jax.ShapeDtypeStruct((RB, T, S), f32),
        ),
        in_specs=[pl.BlockSpec(memory_space=pltpu.SMEM)]
        + [pl.BlockSpec(memory_space=pl.ANY)] * 7,
        out_specs=(vmem, vmem),
        scratch_shapes=[
            pltpu.VMEM((SLOTS, T, T), bf16),
            pltpu.VMEM((CB, T), f32),
            pltpu.VMEM((CB, T), f32),
            pltpu.VMEM((RB, T), jnp.int32),
            pltpu.VMEM((CB, T, S), f32),
            pltpu.VMEM((RB, T, S), f32),
            pltpu.VMEM((2, T, S), f32),
            pltpu.VMEM((RB * T, CB * T), bf16),
            pltpu.VMEM((ITERS + 1, CB, S, T), f32),
            pltpu.VMEM((ITERS + 1, RB, S, T), f32),
            pltpu.VMEM((S, RB * T), bf16),
            pltpu.VMEM((S, CB * T), bf16),
            pltpu.VMEM((ITERS, CB, S, T), f32),
            pltpu.VMEM((ITERS, NQ, CB, H, T), f32),
            pltpu.VMEM((ITERS, NQ, 2, 8, H, T), f32),
            pltpu.VMEM((ITERS, NQ, 2, 8, H, T), f32),
            pltpu.VMEM((ITERS, RB, S, T), f32),
            pltpu.VMEM((ITERS, NQ, 2, 3, 2, H, T), f32),
            pltpu.VMEM((ITERS, NQ, 2, 2, H, T), f32),
            pltpu.VMEM((ITERS, NQ, 2, 3, FR, T), f32),
            pltpu.VMEM((2, S, T), f32),
            dma((8,)),
            dma((ITERS, 2, NQ, 2, 8)),
            dma((ITERS, 2, NQ, 2, 8)),
            dma((ITERS, 2, NQ, 4)),
            dma((ITERS, 2, NQ, 4)),
            dma((ITERS, NQ, 2, 4, 3)),
            dma((ITERS, NQ, 2, 4, 3)),
        ],
        compiler_params=pltpu.CompilerParams(
            collective_id=0, has_side_effects=True, vmem_limit_bytes=56 << 20
        ),
        cost_estimate=pl.CostEstimate(
            flops=8 * SLOTS * T * T * S, bytes_accessed=6 << 20, transcendentals=0
        ),
    )(
        inv,
        tile_values,
        unit_cost,
        capacity,
        demand,
        row_kind,
        primal_start,
        dual_start,
    )


def solution(mesh):
    placed = (
        P(("col", "row"), None, None),
        P(("col", "row")),
        P(("col", "row")),
        P("col", None),
        P("col", None),
        P("row", None, None),
        P("row", None),
        P("col", None, None),
        P("row", None, None),
    )
    return jax.shard_map(
        per_device,
        mesh=mesh,
        in_specs=placed,
        out_specs=(P("col", None, None), P("row", None, None)),
        check_vma=False,
    )
```

```python
import jax
import jax.numpy as jnp
from jax import lax
from jax.experimental import pallas as pl
from jax.experimental.pallas import tpu as pltpu
from jax.sharding import PartitionSpec as P

ITERS = 2
NX, NY, NZ = 4, 4, 16
RB, CB, T, S = 8, 16, 128, 128
NQ = 2
SQ = S // NQ
H = SQ // 2
FR = H // 2
SLOTS = 48

PARENT = {1: 0, 4: 0, 2: 1, 5: 4, 7: 4, 3: 2, 6: 5, 8: 7}
LEVELS = ((0,), (4, 1), (7, 5, 2), (8, 6, 3))
OFFS = (0, 1, -1, 4, -4, 2, -2, 5, -5, 7, -7, 3, -3, 6, -6, 8)
POS = {o: p for p, o in enumerate(OFFS)}
POS[-8] = POS[8]
PARTS = ((0, 5), (5, 11), (11, 16))
GROUPS = ((0, 1), (1, 5), (5, 11), (11, 16))
HOPS = sorted({s * (d - u) for d, u in PARENT.items() for s in (1, -1)})

primal_step = 0.5
dual_step = 0.5


def children(d):
    return [c for c, u in PARENT.items() if u == d]


def half(s, d):
    if d == 8:
        return (0 if s == 1 else H // 2), H // 2
    return 0, H


def kernel(
    inv_ref,
    tiles_hbm,
    cost_hbm,
    cap_hbm,
    demand_hbm,
    kind_hbm,
    primal_hbm,
    dual_hbm,
    primal_out,
    dual_out,
    tiles,
    cost,
    cap,
    kind,
    primal0,
    dual0,
    dem0,
    kd,
    pt,
    dt,
    dl,
    ext,
    ap,
    sib,
    rs_s,
    rs_r,
    fp,
    rx,
    g,
    ry,
    dem,
    local_sem,
    ring_send,
    ring_recv,
    sib_send,
    sib_recv,
    f_send,
    f_recv,
):
    col = lax.axis_index("col")
    row = lax.axis_index("row")
    x, y = lax.div(col, NY), lax.rem(col, NY)
    z, core = lax.div(row, 2), lax.rem(row, 2)
    outer = (x, y)
    inner = (y, x)
    own_at = [pl.multiple_of(q * SQ + core * H, H) for q in range(NQ)]
    oth_at = [pl.multiple_of(q * SQ + (1 - core) * H, H) for q in range(NQ)]
    block_of = [lax.rem(z + OFFS[p] + NZ, NZ) for p in range(CB)]
    z_row = {d: lax.rem(z + d + NZ, NZ) * 2 + core for d in HOPS}
    sibling = (col, z * 2 + 1 - core)
    x_at = [lax.rem(x + d, NX) for d in range(NX)]
    y_at = [lax.rem(y + d, NY) for d in range(NY)]
    outer_at, inner_at = (x_at, y_at), (y_at, x_at)
    x_col = [x_at[d] * NY + y for d in range(NX)]
    y_col = [x * NY + y_at[d] for d in range(NY)]

    def own(q):
        return own_at[q]

    def oth(q):
        return oth_at[q]

    def block_at(p):
        return block_of[p]

    def zdev(d):
        return (col, z_row[d])

    def xdev(d):
        return (x_col[d], row)

    def ydev(d):
        return (y_col[d], row)

    def sub(k):
        return lax.div(k, 2), pl.multiple_of(lax.rem(k, 2) * FR, FR)

    sub_at = [[sub(inner_at[h][d]) for d in range(4)] for h in range(2)]
    dem_block = [2 * outer[h] + sub_at[h][0][0] for h in range(2)]
    loads = [
        pltpu.make_async_copy(src, dst, local_sem.at[n])
        for n, (src, dst) in enumerate(
            [
                (dual_hbm, dual0),
                (tiles_hbm, tiles),
                (primal_hbm, primal0),
                (cost_hbm, cost),
                (cap_hbm, cap),
                (kind_hbm, kind),
                (demand_hbm.at[dem_block[0]], dem0.at[0]),
                (demand_hbm.at[dem_block[1]], dem0.at[1]),
            ]
        )
    ]
    for load in loads:
        load.start()

    barrier = pltpu.get_barrier_semaphore()
    peers = [zdev(d) for d in HOPS] + [sibling]
    peers += [xdev(d) for d in (1, 2, 3)] + [ydev(d) for d in (1, 2, 3)]
    for peer in peers:
        pl.semaphore_signal(
            barrier, inc=1, device_id=peer, device_id_type=pl.DeviceIdType.MESH
        )

    def remote(src, dst, ss, rs, dev):
        return pltpu.make_async_remote_copy(
            src_ref=src,
            dst_ref=dst,
            send_sem=ss,
            recv_sem=rs,
            device_id=dev,
            device_id_type=pl.DeviceIdType.MESH,
        )

    def side(s):
        return 0 if s == 1 else 1

    def rs_copy(it, q, s, d):
        i = (it, q, side(s), d - 1, pl.ds(0, half(s, d)[1]))
        return remote(
            rs_s.at[i], rs_r.at[i], ring_send.at[it, 0, q, side(s), d - 1],
            ring_recv.at[it, 0, q, side(s), d - 1], zdev(s * (d - PARENT[d])),
        )

    def own_rows(q, s, d):
        start, size = half(s, d)
        return pl.ds(pl.multiple_of(own(q) + start, 16), size)

    def ag_copy(it, q, s, d):
        rows = own_rows(q, s, d)
        return remote(
            pt.at[it + 1, POS[-s * PARENT[d]], rows, :],
            pt.at[it + 1, POS[-s * d], rows, :],
            ring_send.at[it, 1, q, side(s), d - 1],
            ring_recv.at[it, 1, q, side(s), d - 1], zdev(s * (d - PARENT[d])),
        )

    def sib_rs(it, q, n):
        lo, hi = PARTS[n]
        return remote(
            ap.at[it, lo:hi, pl.ds(oth(q), H), :], sib.at[it, q, lo:hi],
            sib_send.at[it, 0, q, n], sib_recv.at[it, 0, q, n], sibling,
        )

    def sib_ag(it, q, n, rows):
        lo, hi = GROUPS[n]
        part = pt.at[it + 1, lo:hi, pl.ds(rows, H), :]
        return remote(
            part, part, sib_send.at[it, 1, q, n], sib_recv.at[it, 1, q, n], sibling
        )

    def f_dev(h, d, first):
        return xdev(d) if (h == 0) == first else ydev(d)

    def f_sem(it, q, h, phase, d):
        i = (it, q, h, phase, d - 1)
        return f_send.at[i], f_recv.at[i]

    def f_rs1(it, q, h, d):
        dest = outer_at[h][d]
        return remote(
            fp.at[it, pl.ds(2 * dest, 2), pl.ds(q * SQ + h * H, H), :],
            rx.at[it, q, h, d - 1], *f_sem(it, q, h, 0, d), f_dev(h, d, True),
        )

    def f_rs2(it, q, h, d):
        b, s0 = sub_at[h][d]
        return remote(
            g.at[it, q, h, b, pl.ds(s0, FR), :], ry.at[it, q, h, d - 1],
            *f_sem(it, q, h, 1, d), f_dev(h, d, False),
        )

    def f_rows(q, h, s0):
        return pl.ds(pl.multiple_of(q * SQ + h * H + s0, FR), FR)

    def f_ag1(it, q, h, d, k):
        b, s0 = sub_at[h][k]
        part = dt.at[it + 1, 2 * outer[h] + b, f_rows(q, h, s0), :]
        return remote(part, part, *f_sem(it, q, h, 2, d), f_dev(h, d, False))

    def f_ag2(it, q, h, d, k):
        part = dt.at[it + 1, pl.ds(2 * outer_at[h][k], 2), pl.ds(q * SQ + h * H, H), :]
        return remote(part, part, *f_sem(it, q, h, 3, d), f_dev(h, d, True))

    far_first = (2, 1, 3)

    def build(lo, hi):
        def rows_of(r, _):
            r0 = pl.multiple_of(r * T, T)
            for p in range(lo, hi):
                idx = inv_ref[r * CB + block_at(p)]
                tile = tiles[jnp.maximum(idx, 0)]
                tile = jnp.where(idx >= 0, tile, jnp.zeros_like(tile))
                kd[pl.ds(r0, T), p * T : (p + 1) * T] = tile
            return 0

        lax.fori_loop(0, RB, rows_of, 0)

    def f_ag2_wait(it, q):
        for h in range(2):
            for d in (1, 2, 3):
                f_ag2(it, q, h, d, 4 - d).wait_recv()

    def slab(q):
        return (q * SQ, SQ)

    def iteration(it, _):
        def adjoint(n, rows):
            lo, hi = PARTS[n]
            r0, many = rows
            for p in range(lo, hi, 2):
                w = min(2, hi - p)
                res = jnp.dot(
                    dl[r0 : r0 + many, :],
                    kd[:, p * T : (p + w) * T],
                    preferred_element_type=jnp.float32,
                )
                for k in range(w):
                    ap[it, p + k, r0 : r0 + many] = res[:, k * T : (k + 1) * T]

        def build_first(n):
            @pl.when(it == 0)
            def _():
                build(*PARTS[n])

        def rs_node(q, s, d):
            p = POS[s * d]
            start, size = half(s, d)
            value = (
                ap[it, p, own_rows(q, s, d), :] + sib[it, q, p, start : start + size, :]
            )
            for c in children(d):
                rs_copy(it, q, s, c).wait_recv()
                if c != 8:
                    value = value + rs_r[it, q, side(s), c - 1]
            rs_s[it, q, side(s), d - 1, :size] = value
            if 8 in children(d):
                at, many = half(s, 8)
                rows = slice(at, at + many)
                rs_s[it, q, side(s), d - 1, rows] = (
                    rs_s[it, q, side(s), d - 1, rows] + rs_r[it, q, side(s), 7, :many]
                )
            rs_copy(it, q, s, d).start()

        def rs_level(n, q):
            sib_rs(it, q, n - 1).wait_recv()
            for d in LEVELS[n]:
                for s in (1, -1):
                    rs_node(q, s, d)

        @pl.when(it == 0)
        def _():
            loads[0].wait()
            for b in range(RB):
                dt[0, b] = dual0[b].T
            loads[1].wait()
            build(*PARTS[2])
            pl.semaphore_wait(barrier, len(peers))

        def partial(q, n):
            adjoint(n, slab(q))
            sib_rs(it, q, n).start()

        def begin(q):
            @pl.when(it > 0)
            def _():
                f_ag2_wait(it - 1, q)

            r0, many = slab(q)
            for b in range(RB):
                dl[r0 : r0 + many, b * T : (b + 1) * T] = dt[
                    it, b, r0 : r0 + many
                ].astype(jnp.bfloat16)
            partial(q, 2)

        begin(0)
        build_first(1)
        partial(0, 1)
        begin(1)
        rs_level(3, 0)
        partial(1, 1)
        rs_level(3, 1)
        build_first(0)
        partial(0, 0)
        partial(1, 0)
        for q in range(NQ):
            rs_level(2, q)

        @pl.when(it == 0)
        def _():
            for load in loads[2:]:
                load.wait()
            for p in range(CB):
                pt[0, p] = primal0[block_at(p)].T
            for h in range(2):
                dem[h] = dem0[h].T

        for q in range(NQ):
            rs_level(1, q)

        for q in range(NQ):
            rows = pl.ds(own(q), H)
            total = ap[it, 0, rows, :] + sib[it, q, 0]
            for d in reversed(LEVELS[1]):
                for s in (1, -1):
                    rs_copy(it, q, s, d).wait_recv()
                    total = total + rs_r[it, q, side(s), d - 1]
            old = pt[it, 0, rows, :]
            pt[it + 1, 0, rows, :] = jnp.minimum(
                jnp.maximum(old - primal_step * (cost[pl.ds(z, 1), :] - total), 0.0),
                cap[pl.ds(z, 1), :],
            )
            for d in LEVELS[1]:
                for s in (1, -1):
                    ag_copy(it, q, s, d).start()
            sib_ag(it, q, 0, own(q)).start()

        def ag_level(n, q):
            for d in reversed(LEVELS[n]):
                for s in (1, -1):
                    ag_copy(it, q, s, d).wait_recv()
                    for c in reversed(children(d)):
                        ag_copy(it, q, s, c).start()
            sib_ag(it, q, n, own(q)).start()

        def forward(lo, hi, rows, first):
            r0, many = rows
            at = slice(r0, r0 + many)
            for p in range(lo, hi):
                ext[at, p * T : (p + 1) * T] = (
                    2.0 * pt[it + 1, p, at] - pt[it, p, at]
                ).astype(jnp.bfloat16)
            for n in range(0, RB, 2):
                res = lax.dot_general(
                    ext[at, lo * T : hi * T],
                    kd[n * T : (n + 2) * T, lo * T : hi * T],
                    (((1,), (1,)), ((), ())),
                    preferred_element_type=jnp.float32,
                )
                for k in range(2):
                    part = res[:, k * T : (k + 1) * T]
                    fp[it, n + k, at] = part if first else fp[it, n + k, at] + part

        for n in (1, 2):
            for q in range(NQ):
                ag_level(n, q)
        for q in range(NQ):
            sib_ag(it, q, 0, oth(q)).wait_recv()
            sib_ag(it, q, 1, oth(q)).wait_recv()
            forward(0, 5, slab(q), True)
        for q in range(NQ):
            ag_level(3, q)

        for q in range(NQ):
            sib_ag(it, q, 2, oth(q)).wait_recv()
            forward(5, 11, slab(q), False)
            sib_ag(it, q, 3, oth(q)).wait_recv()
            forward(11, 16, slab(q), False)
            for d in far_first:
                for h in range(2):
                    f_rs1(it, q, h, d).start()

        @pl.when(it == ITERS - 1)
        def _():
            for p in range(CB):
                primal_out[block_at(p)] = pt[ITERS, p].T

        for q in range(NQ):
            for s in (1, -1):
                for d in PARENT:
                    rs_copy(it, q, s, d).wait_send()
                    ag_copy(it, q, s, d).wait_send()
            for n in range(len(GROUPS)):
                sib_ag(it, q, n, own(q)).wait_send()
            for n in range(len(PARTS)):
                sib_rs(it, q, n).wait_send()

        for q in range(NQ):
            for h in range(2):
                for d in (1, 3, 2):
                    f_rs1(it, q, h, d).wait_recv()
                for b in range(2):
                    g[it, q, h, b] = (
                        fp[it, 2 * outer[h] + b, q * SQ + h * H : q * SQ + (h + 1) * H]
                        + rx[it, q, h, 0, b]
                        + rx[it, q, h, 1, b]
                        + rx[it, q, h, 2, b]
                    )
                for d in far_first:
                    f_rs2(it, q, h, d).start()
        for q in range(NQ):
            for h in range(2):
                for d in (1, 3, 2):
                    f_rs2(it, q, h, d).wait_recv()
                b, s0 = sub_at[h][0]
                forward_sum = (
                    g[it, q, h, b, pl.ds(s0, FR), :]
                    + ry[it, q, h, 0]
                    + ry[it, q, h, 1]
                    + ry[it, q, h, 2]
                )
                block = 2 * outer[h] + b
                rows = f_rows(q, h, s0)
                new = dt[it, block, rows, :] + dual_step * (
                    dem[h, rows, :] - forward_sum
                )
                new = jnp.where(
                    kind[pl.ds(block, 1), :] == 1, jnp.maximum(new, 0.0), new
                )
                dt[it + 1, block, rows, :] = new
                for d in far_first:
                    f_ag1(it, q, h, d, 0).start()
        for q in range(NQ):
            for h in range(2):
                for d in (1, 3, 2):
                    f_ag1(it, q, h, d, 4 - d).wait_recv()
                for d in far_first:
                    f_ag2(it, q, h, d, 0).start()
        for q in range(NQ):
            for h in range(2):
                for d in (1, 2, 3):
                    f_rs1(it, q, h, d).wait_send()
                    f_rs2(it, q, h, d).wait_send()
                    f_ag1(it, q, h, d, 0).wait_send()
        return 0

    lax.fori_loop(0, ITERS, iteration, 0)
    for q in range(NQ):
        f_ag2_wait(ITERS - 1, q)
    for b in range(RB):
        dual_out[b] = dt[ITERS, b].T

    for it in range(ITERS):
        for q in range(NQ):
            for h in range(2):
                for d in (1, 2, 3):
                    f_ag2(it, q, h, d, 0).wait_send()


def per_device(
    tile_values,
    tile_row,
    tile_column,
    unit_cost,
    capacity,
    demand,
    row_kind,
    primal_start,
    dual_start,
):
    place = jnp.where(tile_row < RB, tile_row * CB + tile_column, RB * CB)
    slot = jnp.arange(SLOTS, dtype=jnp.int32)
    hit = place[:, None] == jnp.arange(RB * CB, dtype=jnp.int32)[None, :]
    inv = jnp.max(jnp.where(hit, slot[:, None], -1), axis=0)
    vmem = pl.BlockSpec(memory_space=pltpu.VMEM)
    f32, bf16 = jnp.float32, jnp.bfloat16
    dma = pltpu.SemaphoreType.DMA
    return pl.pallas_call(
        kernel,
        out_shape=(
            jax.ShapeDtypeStruct((CB, T, S), f32),
            jax.ShapeDtypeStruct((RB, T, S), f32),
        ),
        in_specs=[pl.BlockSpec(memory_space=pltpu.SMEM)]
        + [pl.BlockSpec(memory_space=pl.ANY)] * 7,
        out_specs=(vmem, vmem),
        scratch_shapes=[
            pltpu.VMEM((SLOTS, T, T), bf16),
            pltpu.VMEM((CB, T), f32),
            pltpu.VMEM((CB, T), f32),
            pltpu.VMEM((RB, T), jnp.int32),
            pltpu.VMEM((CB, T, S), f32),
            pltpu.VMEM((RB, T, S), f32),
            pltpu.VMEM((2, T, S), f32),
            pltpu.VMEM((RB * T, CB * T), bf16),
            pltpu.VMEM((ITERS + 1, CB, S, T), f32),
            pltpu.VMEM((ITERS + 1, RB, S, T), f32),
            pltpu.VMEM((S, RB * T), bf16),
            pltpu.VMEM((S, CB * T), bf16),
            pltpu.VMEM((ITERS, CB, S, T), f32),
            pltpu.VMEM((ITERS, NQ, CB, H, T), f32),
            pltpu.VMEM((ITERS, NQ, 2, 8, H, T), f32),
            pltpu.VMEM((ITERS, NQ, 2, 8, H, T), f32),
            pltpu.VMEM((ITERS, RB, S, T), f32),
            pltpu.VMEM((ITERS, NQ, 2, 3, 2, H, T), f32),
            pltpu.VMEM((ITERS, NQ, 2, 2, H, T), f32),
            pltpu.VMEM((ITERS, NQ, 2, 3, FR, T), f32),
            pltpu.VMEM((2, S, T), f32),
            dma((8,)),
            dma((ITERS, 2, NQ, 2, 8)),
            dma((ITERS, 2, NQ, 2, 8)),
            dma((ITERS, 2, NQ, 4)),
            dma((ITERS, 2, NQ, 4)),
            dma((ITERS, NQ, 2, 4, 3)),
            dma((ITERS, NQ, 2, 4, 3)),
        ],
        compiler_params=pltpu.CompilerParams(
            collective_id=0, has_side_effects=True, vmem_limit_bytes=56 << 20
        ),
        cost_estimate=pl.CostEstimate(
            flops=8 * SLOTS * T * T * S, bytes_accessed=6 << 20, transcendentals=0
        ),
    )(
        inv,
        tile_values,
        unit_cost,
        capacity,
        demand,
        row_kind,
        primal_start,
        dual_start,
    )


def solution(mesh):
    placed = (
        P(("col", "row"), None, None),
        P(("col", "row")),
        P(("col", "row")),
        P("col", None),
        P("col", None),
        P("row", None, None),
        P("row", None),
        P("col", None, None),
        P("row", None, None),
    )
    return jax.shard_map(
        per_device,
        mesh=mesh,
        in_specs=placed,
        out_specs=(P("col", None, None), P("row", None, None)),
        check_vma=False,
    )
```

```python
import jax
import jax.numpy as jnp
from jax import lax
from jax.experimental import pallas as pl
from jax.experimental.pallas import tpu as pltpu
from jax.sharding import PartitionSpec as P

ITERS = 2
NX, NY, NZ = 4, 4, 16
RB, CB, T, S = 8, 16, 128, 128
NQ = 2
SQ = S // NQ
H = SQ // 2
FR = H // 2
SLOTS = 48

PARENT = {1: 0, 4: 0, 2: 1, 5: 4, 7: 4, 3: 2, 6: 5, 8: 7}
LEVELS = ((0,), (4, 1), (7, 5, 2), (8, 6, 3))
OFFS = (0, 1, -1, 4, -4, 2, -2, 5, -5, 7, -7, 3, -3, 6, -6, 8)
POS = {o: p for p, o in enumerate(OFFS)}
POS[-8] = POS[8]
PARTS = ((0, 5), (5, 11), (11, 16))
GROUPS = ((0, 1), (1, 5), (5, 11))
LEAVES = LEVELS[3]
LEAF_HOPS = sorted({s * (d - PARENT[d]) for d in LEAVES for s in (1, -1)})
HOPS = sorted({s * (d - u) for d, u in PARENT.items() for s in (1, -1)})

primal_step = 0.5
dual_step = 0.5


def children(d):
    return [c for c, u in PARENT.items() if u == d]


def half(s, d):
    if d == 8:
        return (0 if s == 1 else H // 2), H // 2
    return 0, H


def kernel(
    inv_ref,
    tiles_hbm,
    cost_hbm,
    cap_hbm,
    demand_hbm,
    kind_hbm,
    primal_hbm,
    dual_hbm,
    primal_out,
    dual_out,
    tiles,
    cost,
    cap,
    kind,
    primal0,
    dual0,
    dem0,
    kd,
    pt,
    dt,
    dl,
    ext,
    ap,
    sib,
    rs_s,
    rs_r,
    rs_x,
    fp,
    rx,
    g,
    ry,
    dem,
    local_sem,
    ring_send,
    ring_recv,
    sib_send,
    sib_recv,
    f_send,
    f_recv,
):
    col = lax.axis_index("col")
    row = lax.axis_index("row")
    x, y = lax.div(col, NY), lax.rem(col, NY)
    z, core = lax.div(row, 2), lax.rem(row, 2)
    outer = (x, y)
    inner = (y, x)
    own_at = [pl.multiple_of(q * SQ + core * H, H) for q in range(NQ)]
    oth_at = [pl.multiple_of(q * SQ + (1 - core) * H, H) for q in range(NQ)]
    block_of = [lax.rem(z + OFFS[p] + NZ, NZ) for p in range(CB)]
    z_row = {d: lax.rem(z + d + NZ, NZ) * 2 + core for d in HOPS}
    cross_row = {d: lax.rem(z + d + NZ, NZ) * 2 + 1 - core for d in LEAF_HOPS}
    sibling = (col, z * 2 + 1 - core)
    x_at = [lax.rem(x + d, NX) for d in range(NX)]
    y_at = [lax.rem(y + d, NY) for d in range(NY)]
    outer_at, inner_at = (x_at, y_at), (y_at, x_at)
    x_col = [x_at[d] * NY + y for d in range(NX)]
    y_col = [x * NY + y_at[d] for d in range(NY)]

    def own(q):
        return own_at[q]

    def oth(q):
        return oth_at[q]

    def block_at(p):
        return block_of[p]

    def zdev(d):
        return (col, z_row[d])

    def xdev(d):
        return (x_col[d], row)

    def ydev(d):
        return (y_col[d], row)

    def sub(k):
        return lax.div(k, 2), pl.multiple_of(lax.rem(k, 2) * FR, FR)

    sub_at = [[sub(inner_at[h][d]) for d in range(4)] for h in range(2)]
    dem_block = [2 * outer[h] + sub_at[h][0][0] for h in range(2)]
    loads = [
        pltpu.make_async_copy(src, dst, local_sem.at[n])
        for n, (src, dst) in enumerate(
            [
                (dual_hbm, dual0),
                (tiles_hbm, tiles),
                (primal_hbm, primal0),
                (cost_hbm, cost),
                (cap_hbm, cap),
                (kind_hbm, kind),
                (demand_hbm.at[dem_block[0]], dem0.at[0]),
                (demand_hbm.at[dem_block[1]], dem0.at[1]),
            ]
        )
    ]
    for load in loads:
        load.start()

    barrier = pltpu.get_barrier_semaphore()
    peers = [zdev(d) for d in HOPS] + [sibling]
    peers += [(col, cross_row[d]) for d in LEAF_HOPS]
    peers += [xdev(d) for d in (1, 2, 3)] + [ydev(d) for d in (1, 2, 3)]
    for peer in peers:
        pl.semaphore_signal(
            barrier, inc=1, device_id=peer, device_id_type=pl.DeviceIdType.MESH
        )

    def remote(src, dst, ss, rs, dev):
        return pltpu.make_async_remote_copy(
            src_ref=src,
            dst_ref=dst,
            send_sem=ss,
            recv_sem=rs,
            device_id=dev,
            device_id_type=pl.DeviceIdType.MESH,
        )

    def side(s):
        return 0 if s == 1 else 1

    def rs_copy(it, q, s, d):
        i = (it, q, side(s), d - 1, pl.ds(0, half(s, d)[1]))
        return remote(
            rs_s.at[i], rs_r.at[i], ring_send.at[it, 0, q, side(s), d - 1],
            ring_recv.at[it, 0, q, side(s), d - 1], zdev(s * (d - PARENT[d])),
        )

    def rows_at(first, s, d):
        start, size = half(s, d)
        return pl.ds(pl.multiple_of(first + start, 16), size)

    def own_rows(q, s, d):
        return rows_at(own(q), s, d)

    def rs_leaf(it, q, s, d, cross):
        hop = s * (d - PARENT[d])
        phase, into = (2, rs_x) if cross else (0, rs_r)
        rows = rows_at(oth(q) if cross else own(q), s, d)
        return remote(
            ap.at[it, POS[s * d], rows, :],
            into.at[it, q, side(s), d - 1, pl.ds(0, half(s, d)[1])],
            ring_send.at[it, phase, q, side(s), d - 1],
            ring_recv.at[it, phase, q, side(s), d - 1],
            (col, cross_row[hop] if cross else z_row[hop]),
        )

    def ag_copy(it, q, s, d, cross=False, arrival=False):
        hop = s * (d - PARENT[d])
        phase = 3 if cross else 1
        rows = rows_at(oth(q) if cross and arrival else own(q), s, d)
        return remote(
            pt.at[it + 1, POS[-s * PARENT[d]], rows, :],
            pt.at[it + 1, POS[-s * d], rows, :],
            ring_send.at[it, phase, q, side(s), d - 1],
            ring_recv.at[it, phase, q, side(s), d - 1],
            (col, cross_row[hop] if cross else z_row[hop]),
        )

    def sib_rs(it, q, n):
        lo, hi = PARTS[n]
        return remote(
            ap.at[it, lo:hi, pl.ds(oth(q), H), :], sib.at[it, q, lo:hi],
            sib_send.at[it, 0, q, n], sib_recv.at[it, 0, q, n], sibling,
        )

    def sib_ag(it, q, n, rows):
        lo, hi = GROUPS[n]
        part = pt.at[it + 1, lo:hi, pl.ds(rows, H), :]
        return remote(
            part, part, sib_send.at[it, 1, q, n], sib_recv.at[it, 1, q, n], sibling
        )

    def f_dev(h, d, first):
        return xdev(d) if (h == 0) == first else ydev(d)

    def f_sem(it, q, h, phase, d):
        i = (it, q, h, phase, d - 1)
        return f_send.at[i], f_recv.at[i]

    def f_rs1(it, q, h, d):
        dest = outer_at[h][d]
        return remote(
            fp.at[it, pl.ds(2 * dest, 2), pl.ds(q * SQ + h * H, H), :],
            rx.at[it, q, h, d - 1], *f_sem(it, q, h, 0, d), f_dev(h, d, True),
        )

    def f_rs2(it, q, h, d):
        b, s0 = sub_at[h][d]
        return remote(
            g.at[it, q, h, b, pl.ds(s0, FR), :], ry.at[it, q, h, d - 1],
            *f_sem(it, q, h, 1, d), f_dev(h, d, False),
        )

    def f_rows(q, h, s0):
        return pl.ds(pl.multiple_of(q * SQ + h * H + s0, FR), FR)

    def f_ag1(it, q, h, d, k):
        b, s0 = sub_at[h][k]
        part = dt.at[it + 1, 2 * outer[h] + b, f_rows(q, h, s0), :]
        return remote(part, part, *f_sem(it, q, h, 2, d), f_dev(h, d, False))

    def f_ag2(it, q, h, d, k):
        part = dt.at[it + 1, pl.ds(2 * outer_at[h][k], 2), pl.ds(q * SQ + h * H, H), :]
        return remote(part, part, *f_sem(it, q, h, 3, d), f_dev(h, d, True))

    far_first = (2, 1, 3)

    def build(lo, hi):
        def rows_of(r, _):
            r0 = pl.multiple_of(r * T, T)
            for p in range(lo, hi):
                idx = inv_ref[r * CB + block_at(p)]
                tile = tiles[jnp.maximum(idx, 0)]
                tile = jnp.where(idx >= 0, tile, jnp.zeros_like(tile))
                kd[pl.ds(r0, T), p * T : (p + 1) * T] = tile
            return 0

        lax.fori_loop(0, RB, rows_of, 0)

    def f_ag2_wait(it, q):
        for h in range(2):
            for d in (1, 2, 3):
                f_ag2(it, q, h, d, 4 - d).wait_recv()

    def slab(q):
        return (q * SQ, SQ)

    def iteration(it, _):
        def adjoint(n, rows):
            lo, hi = PARTS[n]
            r0, many = rows
            for p in range(lo, hi, 2):
                w = min(2, hi - p)
                res = jnp.dot(
                    dl[r0 : r0 + many, :],
                    kd[:, p * T : (p + w) * T],
                    preferred_element_type=jnp.float32,
                )
                for k in range(w):
                    ap[it, p + k, r0 : r0 + many] = res[:, k * T : (k + 1) * T]

        def build_first(n):
            @pl.when(it == 0)
            def _():
                build(*PARTS[n])

        def rs_node(q, s, d):
            p = POS[s * d]
            start, size = half(s, d)
            value = (
                ap[it, p, own_rows(q, s, d), :] + sib[it, q, p, start : start + size, :]
            )
            for c in children(d):
                if c in LEAVES:
                    rs_leaf(it, q, s, c, False).wait_recv()
                    rs_leaf(it, q, s, c, True).wait_recv()
                else:
                    rs_copy(it, q, s, c).wait_recv()
                if c != 8:
                    value = value + rs_r[it, q, side(s), c - 1]
                if c in (3, 6):
                    value = value + rs_x[it, q, side(s), c - 1]
            rs_s[it, q, side(s), d - 1, :size] = value
            if 8 in children(d):
                at, many = half(s, 8)
                rows = slice(at, at + many)
                rs_s[it, q, side(s), d - 1, rows] = (
                    rs_s[it, q, side(s), d - 1, rows]
                    + rs_r[it, q, side(s), 7, :many]
                    + rs_x[it, q, side(s), 7, :many]
                )
            rs_copy(it, q, s, d).start()

        def rs_level(n, q):
            sib_rs(it, q, n - 1).wait_recv()
            for d in LEVELS[n]:
                for s in (1, -1):
                    rs_node(q, s, d)

        @pl.when(it == 0)
        def _():
            loads[0].wait()
            for b in range(RB):
                dt[0, b] = dual0[b].T
            loads[1].wait()
            build(*PARTS[2])
            pl.semaphore_wait(barrier, len(peers))

        def partial(q, n):
            adjoint(n, slab(q))
            sib_rs(it, q, n).start()

        def begin(q):
            @pl.when(it > 0)
            def _():
                f_ag2_wait(it - 1, q)

            r0, many = slab(q)
            for b in range(RB):
                dl[r0 : r0 + many, b * T : (b + 1) * T] = dt[
                    it, b, r0 : r0 + many
                ].astype(jnp.bfloat16)
            adjoint(2, slab(q))
            for d in LEAVES:
                for s in (1, -1):
                    rs_leaf(it, q, s, d, False).start()
                    rs_leaf(it, q, s, d, True).start()

        begin(0)
        build_first(1)
        partial(0, 1)
        begin(1)
        partial(1, 1)
        build_first(0)
        partial(0, 0)
        partial(1, 0)
        for q in range(NQ):
            rs_level(2, q)

        @pl.when(it == 0)
        def _():
            for load in loads[2:]:
                load.wait()
            for p in range(CB):
                pt[0, p] = primal0[block_at(p)].T
            for h in range(2):
                dem[h] = dem0[h].T

        for q in range(NQ):
            rs_level(1, q)

        for q in range(NQ):
            rows = pl.ds(own(q), H)
            total = ap[it, 0, rows, :] + sib[it, q, 0]
            for d in reversed(LEVELS[1]):
                for s in (1, -1):
                    rs_copy(it, q, s, d).wait_recv()
                    total = total + rs_r[it, q, side(s), d - 1]
            old = pt[it, 0, rows, :]
            pt[it + 1, 0, rows, :] = jnp.minimum(
                jnp.maximum(old - primal_step * (cost[pl.ds(z, 1), :] - total), 0.0),
                cap[pl.ds(z, 1), :],
            )
            for d in LEVELS[1]:
                for s in (1, -1):
                    ag_copy(it, q, s, d).start()
            sib_ag(it, q, 0, own(q)).start()

        def ag_level(n, q):
            for d in reversed(LEVELS[n]):
                for s in (1, -1):
                    ag_copy(it, q, s, d).wait_recv()
                    for c in reversed(children(d)):
                        ag_copy(it, q, s, c).start()
                        if c in LEAVES:
                            ag_copy(it, q, s, c, True).start()
            sib_ag(it, q, n, own(q)).start()

        def forward(lo, hi, rows, first):
            r0, many = rows
            at = slice(r0, r0 + many)
            for p in range(lo, hi):
                ext[at, p * T : (p + 1) * T] = (
                    2.0 * pt[it + 1, p, at] - pt[it, p, at]
                ).astype(jnp.bfloat16)
            for n in range(0, RB, 2):
                res = lax.dot_general(
                    ext[at, lo * T : hi * T],
                    kd[n * T : (n + 2) * T, lo * T : hi * T],
                    (((1,), (1,)), ((), ())),
                    preferred_element_type=jnp.float32,
                )
                for k in range(2):
                    part = res[:, k * T : (k + 1) * T]
                    fp[it, n + k, at] = part if first else fp[it, n + k, at] + part

        for n in (1, 2):
            for q in range(NQ):
                ag_level(n, q)
        for q in range(NQ):
            sib_ag(it, q, 0, oth(q)).wait_recv()
            sib_ag(it, q, 1, oth(q)).wait_recv()
            forward(0, 5, slab(q), True)
        for q in range(NQ):
            sib_ag(it, q, 2, oth(q)).wait_recv()
            forward(5, 11, slab(q), False)
            for d in LEAVES:
                for s in (1, -1):
                    ag_copy(it, q, s, d).wait_recv()
                    ag_copy(it, q, s, d, True, True).wait_recv()
            forward(11, 16, slab(q), False)
            for d in far_first:
                for h in range(2):
                    f_rs1(it, q, h, d).start()

        @pl.when(it == ITERS - 1)
        def _():
            for p in range(CB):
                primal_out[block_at(p)] = pt[ITERS, p].T

        for q in range(NQ):
            for s in (1, -1):
                for d in PARENT:
                    ag_copy(it, q, s, d).wait_send()
                    if d in LEAVES:
                        ag_copy(it, q, s, d, True).wait_send()
                        rs_leaf(it, q, s, d, False).wait_send()
                        rs_leaf(it, q, s, d, True).wait_send()
                    else:
                        rs_copy(it, q, s, d).wait_send()
            for n in range(len(GROUPS)):
                sib_ag(it, q, n, own(q)).wait_send()
            for n in range(2):
                sib_rs(it, q, n).wait_send()

        for q in range(NQ):
            for h in range(2):
                for d in (1, 3, 2):
                    f_rs1(it, q, h, d).wait_recv()
                for b in range(2):
                    g[it, q, h, b] = (
                        fp[it, 2 * outer[h] + b, q * SQ + h * H : q * SQ + (h + 1) * H]
                        + rx[it, q, h, 0, b]
                        + rx[it, q, h, 1, b]
                        + rx[it, q, h, 2, b]
                    )
                for d in far_first:
                    f_rs2(it, q, h, d).start()
        for q in range(NQ):
            for h in range(2):
                for d in (1, 3, 2):
                    f_rs2(it, q, h, d).wait_recv()
                b, s0 = sub_at[h][0]
                forward_sum = (
                    g[it, q, h, b, pl.ds(s0, FR), :]
                    + ry[it, q, h, 0]
                    + ry[it, q, h, 1]
                    + ry[it, q, h, 2]
                )
                block = 2 * outer[h] + b
                rows = f_rows(q, h, s0)
                new = dt[it, block, rows, :] + dual_step * (
                    dem[h, rows, :] - forward_sum
                )
                new = jnp.where(
                    kind[pl.ds(block, 1), :] == 1, jnp.maximum(new, 0.0), new
                )
                dt[it + 1, block, rows, :] = new
                for d in far_first:
                    f_ag1(it, q, h, d, 0).start()
        for q in range(NQ):
            for h in range(2):
                for d in (1, 3, 2):
                    f_ag1(it, q, h, d, 4 - d).wait_recv()
                for d in far_first:
                    f_ag2(it, q, h, d, 0).start()
        for q in range(NQ):
            for h in range(2):
                for d in (1, 2, 3):
                    f_rs1(it, q, h, d).wait_send()
                    f_rs2(it, q, h, d).wait_send()
                    f_ag1(it, q, h, d, 0).wait_send()
        return 0

    lax.fori_loop(0, ITERS, iteration, 0)
    for q in range(NQ):
        f_ag2_wait(ITERS - 1, q)
    for b in range(RB):
        dual_out[b] = dt[ITERS, b].T

    for it in range(ITERS):
        for q in range(NQ):
            for h in range(2):
                for d in (1, 2, 3):
                    f_ag2(it, q, h, d, 0).wait_send()


def per_device(
    tile_values,
    tile_row,
    tile_column,
    unit_cost,
    capacity,
    demand,
    row_kind,
    primal_start,
    dual_start,
):
    place = jnp.where(tile_row < RB, tile_row * CB + tile_column, RB * CB)
    slot = jnp.arange(SLOTS, dtype=jnp.int32)
    hit = place[:, None] == jnp.arange(RB * CB, dtype=jnp.int32)[None, :]
    inv = jnp.max(jnp.where(hit, slot[:, None], -1), axis=0)
    vmem = pl.BlockSpec(memory_space=pltpu.VMEM)
    f32, bf16 = jnp.float32, jnp.bfloat16
    dma = pltpu.SemaphoreType.DMA
    return pl.pallas_call(
        kernel,
        out_shape=(
            jax.ShapeDtypeStruct((CB, T, S), f32),
            jax.ShapeDtypeStruct((RB, T, S), f32),
        ),
        in_specs=[pl.BlockSpec(memory_space=pltpu.SMEM)]
        + [pl.BlockSpec(memory_space=pl.ANY)] * 7,
        out_specs=(vmem, vmem),
        scratch_shapes=[
            pltpu.VMEM((SLOTS, T, T), bf16),
            pltpu.VMEM((CB, T), f32),
            pltpu.VMEM((CB, T), f32),
            pltpu.VMEM((RB, T), jnp.int32),
            pltpu.VMEM((CB, T, S), f32),
            pltpu.VMEM((RB, T, S), f32),
            pltpu.VMEM((2, T, S), f32),
            pltpu.VMEM((RB * T, CB * T), bf16),
            pltpu.VMEM((ITERS + 1, CB, S, T), f32),
            pltpu.VMEM((ITERS + 1, RB, S, T), f32),
            pltpu.VMEM((S, RB * T), bf16),
            pltpu.VMEM((S, CB * T), bf16),
            pltpu.VMEM((ITERS, CB, S, T), f32),
            pltpu.VMEM((ITERS, NQ, CB, H, T), f32),
            pltpu.VMEM((ITERS, NQ, 2, 8, H, T), f32),
            pltpu.VMEM((ITERS, NQ, 2, 8, H, T), f32),
            pltpu.VMEM((ITERS, NQ, 2, 8, H, T), f32),
            pltpu.VMEM((ITERS, RB, S, T), f32),
            pltpu.VMEM((ITERS, NQ, 2, 3, 2, H, T), f32),
            pltpu.VMEM((ITERS, NQ, 2, 2, H, T), f32),
            pltpu.VMEM((ITERS, NQ, 2, 3, FR, T), f32),
            pltpu.VMEM((2, S, T), f32),
            dma((8,)),
            dma((ITERS, 4, NQ, 2, 8)),
            dma((ITERS, 4, NQ, 2, 8)),
            dma((ITERS, 2, NQ, 4)),
            dma((ITERS, 2, NQ, 4)),
            dma((ITERS, NQ, 2, 4, 3)),
            dma((ITERS, NQ, 2, 4, 3)),
        ],
        compiler_params=pltpu.CompilerParams(
            collective_id=0, has_side_effects=True, vmem_limit_bytes=56 << 20
        ),
        cost_estimate=pl.CostEstimate(
            flops=8 * SLOTS * T * T * S, bytes_accessed=6 << 20, transcendentals=0
        ),
    )(
        inv,
        tile_values,
        unit_cost,
        capacity,
        demand,
        row_kind,
        primal_start,
        dual_start,
    )


def solution(mesh):
    placed = (
        P(("col", "row"), None, None),
        P(("col", "row")),
        P(("col", "row")),
        P("col", None),
        P("col", None),
        P("row", None, None),
        P("row", None),
        P("col", None, None),
        P("row", None, None),
    )
    return jax.shard_map(
        per_device,
        mesh=mesh,
        in_specs=placed,
        out_specs=(P("col", None, None), P("row", None, None)),
        check_vma=False,
    )
```

```python
import jax
import jax.numpy as jnp
from jax import lax
from jax.experimental import pallas as pl
from jax.experimental.pallas import tpu as pltpu
from jax.sharding import PartitionSpec as P

ITERS = 2
NX, NY, NZ = 4, 4, 16
RB, CB, T, S = 8, 16, 128, 128
NQ = 2
SQ = S // NQ
H = SQ // 2
FR = SQ // 2
SLOTS = 48

PARENT = {1: 0, 4: 0, 2: 1, 5: 4, 7: 4, 3: 2, 6: 5, 8: 7}
LEVELS = ((0,), (4, 1), (7, 5, 2), (8, 6, 3))
OFFS = (0, 1, -1, 4, -4, 2, -2, 5, -5, 7, -7, 3, -3, 6, -6, 8)
POS = {o: p for p, o in enumerate(OFFS)}
POS[-8] = POS[8]
PARTS = ((0, 5), (5, 11), (11, 16))
GROUPS = ((0, 1), (1, 5), (5, 11))
LEAVES = LEVELS[3]
LEAF_HOPS = sorted({s * (d - PARENT[d]) for d in LEAVES for s in (1, -1)})
HOPS = sorted({s * (d - u) for d, u in PARENT.items() for s in (1, -1)})

PLANE = sorted(
    [(a, b) for a in range(NX) for b in range(NY) if a or b],
    key=lambda o: -(min(o[0], NX - o[0]) + min(o[1], NY - o[1])),
)

primal_step = 0.5
dual_step = 0.5


def children(d):
    return [c for c, u in PARENT.items() if u == d]


def half(s, d):
    if d == 8:
        return (0 if s == 1 else H // 2), H // 2
    return 0, H


def kernel(
    inv_ref,
    tiles_hbm,
    cost_hbm,
    cap_hbm,
    demand_hbm,
    kind_hbm,
    primal_hbm,
    dual_hbm,
    primal_out,
    dual_out,
    tiles,
    cost,
    cap,
    kind,
    primal0,
    dual0,
    dem0,
    kd,
    pt,
    dt,
    dl,
    ext,
    ap,
    sib,
    rs_s,
    rs_r,
    rs_x,
    fp,
    rx,
    dem,
    local_sem,
    ring_send,
    ring_recv,
    sib_send,
    sib_recv,
    f_send,
    f_recv,
):
    col = lax.axis_index("col")
    row = lax.axis_index("row")
    x, y = lax.div(col, NY), lax.rem(col, NY)
    z, core = lax.div(row, 2), lax.rem(row, 2)
    own_at = [pl.multiple_of(q * SQ + core * H, H) for q in range(NQ)]
    oth_at = [pl.multiple_of(q * SQ + (1 - core) * H, H) for q in range(NQ)]
    block_of = [lax.rem(z + OFFS[p] + NZ, NZ) for p in range(CB)]
    z_row = {d: lax.rem(z + d + NZ, NZ) * 2 + core for d in HOPS}
    cross_row = {d: lax.rem(z + d + NZ, NZ) * 2 + 1 - core for d in LEAF_HOPS}
    sibling = (col, z * 2 + 1 - core)
    x_at = [lax.rem(x + d, NX) for d in range(NX)]
    y_at = [lax.rem(y + d, NY) for d in range(NY)]
    plane_at = {
        (a, b): x_at[a] * NY + y_at[b] for a in range(NX) for b in range(NY)
    }
    block_own = lax.div(col, 2)

    def own(q):
        return own_at[q]

    def oth(q):
        return oth_at[q]

    def block_at(p):
        return block_of[p]

    def zdev(d):
        return (col, z_row[d])

    loads = [
        pltpu.make_async_copy(src, dst, local_sem.at[n])
        for n, (src, dst) in enumerate(
            [
                (dual_hbm, dual0),
                (tiles_hbm, tiles),
                (primal_hbm, primal0),
                (cost_hbm, cost),
                (cap_hbm, cap),
                (kind_hbm, kind),
                (demand_hbm.at[block_own], dem0),
            ]
        )
    ]
    for load in loads:
        load.start()

    barrier = pltpu.get_barrier_semaphore()
    peers = [zdev(d) for d in HOPS] + [sibling]
    peers += [(col, cross_row[d]) for d in LEAF_HOPS]
    peers += [(plane_at[o], row) for o in PLANE]
    for peer in peers:
        pl.semaphore_signal(
            barrier, inc=1, device_id=peer, device_id_type=pl.DeviceIdType.MESH
        )

    def remote(src, dst, ss, rs, dev):
        return pltpu.make_async_remote_copy(
            src_ref=src,
            dst_ref=dst,
            send_sem=ss,
            recv_sem=rs,
            device_id=dev,
            device_id_type=pl.DeviceIdType.MESH,
        )

    def side(s):
        return 0 if s == 1 else 1

    def rs_copy(it, q, s, d):
        i = (it, q, side(s), d - 1, pl.ds(0, half(s, d)[1]))
        return remote(
            rs_s.at[i], rs_r.at[i], ring_send.at[it, 0, q, side(s), d - 1],
            ring_recv.at[it, 0, q, side(s), d - 1], zdev(s * (d - PARENT[d])),
        )

    def rows_at(first, s, d):
        start, size = half(s, d)
        return pl.ds(pl.multiple_of(first + start, 16), size)

    def own_rows(q, s, d):
        return rows_at(own(q), s, d)

    def rs_leaf(it, q, s, d, cross):
        hop = s * (d - PARENT[d])
        phase, into = (2, rs_x) if cross else (0, rs_r)
        rows = rows_at(oth(q) if cross else own(q), s, d)
        return remote(
            ap.at[it, POS[s * d], rows, :],
            into.at[it, q, side(s), d - 1, pl.ds(0, half(s, d)[1])],
            ring_send.at[it, phase, q, side(s), d - 1],
            ring_recv.at[it, phase, q, side(s), d - 1],
            (col, cross_row[hop] if cross else z_row[hop]),
        )

    def ag_copy(it, q, s, d, cross=False, arrival=False):
        hop = s * (d - PARENT[d])
        phase = 3 if cross else 1
        rows = rows_at(oth(q) if cross and arrival else own(q), s, d)
        return remote(
            pt.at[it + 1, POS[-s * PARENT[d]], rows, :],
            pt.at[it + 1, POS[-s * d], rows, :],
            ring_send.at[it, phase, q, side(s), d - 1],
            ring_recv.at[it, phase, q, side(s), d - 1],
            (col, cross_row[hop] if cross else z_row[hop]),
        )

    def sib_rs(it, q, n):
        lo, hi = PARTS[n]
        return remote(
            ap.at[it, lo:hi, pl.ds(oth(q), H), :], sib.at[it, q, lo:hi],
            sib_send.at[it, 0, q, n], sib_recv.at[it, 0, q, n], sibling,
        )

    def sib_ag(it, q, n, rows):
        lo, hi = GROUPS[n]
        part = pt.at[it + 1, lo:hi, pl.ds(rows, H), :]
        return remote(
            part, part, sib_send.at[it, 1, q, n], sib_recv.at[it, 1, q, n], sibling
        )

    def chunk(q, k):
        return lax.div(k, 2), pl.ds(
            pl.multiple_of(q * SQ + lax.rem(k, 2) * FR, FR), FR
        )

    def back(o):
        return (NX - o[0]) % NX, (NY - o[1]) % NY

    def f_rs(it, q, j):
        k = plane_at[PLANE[j]]
        block, rows = chunk(q, k)
        return remote(
            fp.at[it, block, rows, :], rx.at[it, q, j],
            f_send.at[it, q, 0, j], f_recv.at[it, q, 0, j], (k, row),
        )

    def f_ag(it, q, j, arrival=False):
        block, rows = chunk(q, plane_at[back(PLANE[j])] if arrival else col)
        part = dt.at[it + 1, block, rows, :]
        return remote(
            part, part, f_send.at[it, q, 1, j], f_recv.at[it, q, 1, j],
            (plane_at[PLANE[j]], row),
        )

    others = range(len(PLANE))
    near_first = tuple(reversed(others))

    def build(lo, hi):
        def rows_of(r, _):
            r0 = pl.multiple_of(r * T, T)
            for p in range(lo, hi):
                idx = inv_ref[r, block_at(p)]
                tile = tiles[jnp.maximum(idx, 0)]
                tile = jnp.where(idx >= 0, tile, jnp.zeros_like(tile))
                kd[pl.ds(r0, T), p * T : (p + 1) * T] = tile
            return 0

        lax.fori_loop(0, RB, rows_of, 0)

    def f_ag_wait(it, q):
        for j in near_first:
            f_ag(it, q, j, True).wait_recv()

    def slab(q):
        return (q * SQ, SQ)

    def iteration(it, _):
        def adjoint(lo, hi, rows):
            r0, many = rows
            for p in range(lo, hi, 2):
                w = min(2, hi - p)
                res = jnp.dot(
                    dl[r0 : r0 + many, :],
                    kd[:, p * T : (p + w) * T],
                    preferred_element_type=jnp.float32,
                )
                for k in range(w):
                    ap[it, p + k, r0 : r0 + many] = res[:, k * T : (k + 1) * T]

        def build_first(n):
            @pl.when(it == 0)
            def _():
                build(*PARTS[n])

        def rs_node(q, s, d):
            p = POS[s * d]
            start, size = half(s, d)
            value = (
                ap[it, p, own_rows(q, s, d), :] + sib[it, q, p, start : start + size, :]
            )
            for c in children(d):
                if c in LEAVES:
                    rs_leaf(it, q, s, c, False).wait_recv()
                    rs_leaf(it, q, s, c, True).wait_recv()
                else:
                    rs_copy(it, q, s, c).wait_recv()
                if c != 8:
                    value = value + rs_r[it, q, side(s), c - 1]
                if c in (3, 6):
                    value = value + rs_x[it, q, side(s), c - 1]
            rs_s[it, q, side(s), d - 1, :size] = value
            if 8 in children(d):
                at, many = half(s, 8)
                rows = slice(at, at + many)
                rs_s[it, q, side(s), d - 1, rows] = (
                    rs_s[it, q, side(s), d - 1, rows]
                    + rs_r[it, q, side(s), 7, :many]
                    + rs_x[it, q, side(s), 7, :many]
                )
            rs_copy(it, q, s, d).start()

        def rs_level(n, q):
            sib_rs(it, q, n - 1).wait_recv()
            for d in LEVELS[n]:
                for s in (1, -1):
                    rs_node(q, s, d)

        @pl.when(it == 0)
        def _():
            loads[0].wait()
            for b in range(RB):
                dl[:, b * T : (b + 1) * T] = dual0[b].astype(jnp.bfloat16).T
            loads[1].wait()
            build(*PARTS[2])
            pl.semaphore_wait(barrier, len(peers))

        def partial(q, n):
            adjoint(*PARTS[n], slab(q))
            sib_rs(it, q, n).start()

        def begin(q):
            @pl.when(it > 0)
            def _():
                f_ag_wait(it - 1, q)
                r0, many = slab(q)
                for b in range(RB):
                    dl[r0 : r0 + many, b * T : (b + 1) * T] = dt[
                        it, b, r0 : r0 + many
                    ].astype(jnp.bfloat16)

            for d in LEAVES:
                at = sorted({POS[d], POS[-d]})
                adjoint(at[0], at[-1] + 1, slab(q))
                for s in (1, -1):
                    rs_leaf(it, q, s, d, False).start()
                    rs_leaf(it, q, s, d, True).start()

        begin(0)
        build_first(1)
        partial(0, 1)
        begin(1)
        partial(1, 1)
        build_first(0)
        partial(0, 0)
        partial(1, 0)
        for q in range(NQ):
            rs_level(2, q)

        @pl.when(it == 0)
        def _():
            for load in loads[2:]:
                load.wait()
            for p in range(CB):
                pt[0, p] = primal0[block_at(p)].T
            for b in range(RB):
                dt[0, b] = dual0[b].T
            dem[...] = dem0[...].T

        for q in range(NQ):
            rs_level(1, q)

        for q in range(NQ):
            rows = pl.ds(own(q), H)
            total = ap[it, 0, rows, :] + sib[it, q, 0]
            for d in reversed(LEVELS[1]):
                for s in (1, -1):
                    rs_copy(it, q, s, d).wait_recv()
                    total = total + rs_r[it, q, side(s), d - 1]
            old = pt[it, 0, rows, :]
            pt[it + 1, 0, rows, :] = jnp.minimum(
                jnp.maximum(old - primal_step * (cost[pl.ds(z, 1), :] - total), 0.0),
                cap[pl.ds(z, 1), :],
            )
            for d in LEVELS[1]:
                for s in (1, -1):
                    ag_copy(it, q, s, d).start()
            sib_ag(it, q, 0, own(q)).start()

        def ag_level(n, q):
            for d in reversed(LEVELS[n]):
                for s in (1, -1):
                    ag_copy(it, q, s, d).wait_recv()
                    for c in reversed(children(d)):
                        ag_copy(it, q, s, c).start()
                        if c in LEAVES:
                            ag_copy(it, q, s, c, True).start()
            sib_ag(it, q, n, own(q)).start()

        def forward(lo, hi, rows, first):
            r0, many = rows
            at = slice(r0, r0 + many)
            for p in range(lo, hi):
                ext[at, p * T : (p + 1) * T] = (
                    2.0 * pt[it + 1, p, at] - pt[it, p, at]
                ).astype(jnp.bfloat16)
            for n in range(0, RB, 2):
                res = lax.dot_general(
                    ext[at, lo * T : hi * T],
                    kd[n * T : (n + 2) * T, lo * T : hi * T],
                    (((1,), (1,)), ((), ())),
                    preferred_element_type=jnp.float32,
                )
                for k in range(2):
                    part = res[:, k * T : (k + 1) * T]
                    fp[it, n + k, at] = part if first else fp[it, n + k, at] + part

        for n in (1, 2):
            for q in range(NQ):
                ag_level(n, q)
        for q in range(NQ):
            sib_ag(it, q, 0, oth(q)).wait_recv()
            sib_ag(it, q, 1, oth(q)).wait_recv()
            forward(0, 5, slab(q), True)
        for q in range(NQ):
            sib_ag(it, q, 2, oth(q)).wait_recv()
            forward(5, 11, slab(q), False)
            for d in LEAVES:
                for s in (1, -1):
                    ag_copy(it, q, s, d).wait_recv()
                    ag_copy(it, q, s, d, True, True).wait_recv()
            forward(11, 16, slab(q), False)
            for j in others:
                f_rs(it, q, j).start()

        @pl.when(it == ITERS - 1)
        def _():
            for p in range(CB):
                primal_out[block_at(p)] = pt[ITERS, p].T

        for q in range(NQ):
            for s in (1, -1):
                for d in PARENT:
                    ag_copy(it, q, s, d).wait_send()
                    if d in LEAVES:
                        ag_copy(it, q, s, d, True).wait_send()
                        rs_leaf(it, q, s, d, False).wait_send()
                        rs_leaf(it, q, s, d, True).wait_send()
                    else:
                        rs_copy(it, q, s, d).wait_send()
            for n in range(len(GROUPS)):
                sib_ag(it, q, n, own(q)).wait_send()
            for n in range(2):
                sib_rs(it, q, n).wait_send()

        for q in range(NQ):
            block, rows = chunk(q, col)
            forward_sum = fp[it, block, rows, :]
            for j in near_first:
                f_rs(it, q, j).wait_recv()
                forward_sum = forward_sum + rx[it, q, j]
            new = dt[it, block, rows, :] + dual_step * (dem[rows, :] - forward_sum)
            new = jnp.where(kind[pl.ds(block, 1), :] == 1, jnp.maximum(new, 0.0), new)
            dt[it + 1, block, rows, :] = new
            for j in others:
                f_ag(it, q, j).start()
        for q in range(NQ):
            for j in others:
                f_rs(it, q, j).wait_send()
        return 0

    lax.fori_loop(0, ITERS, iteration, 0)
    for q in range(NQ):
        f_ag_wait(ITERS - 1, q)
    for b in range(RB):
        dual_out[b] = dt[ITERS, b].T

    for it in range(ITERS):
        for q in range(NQ):
            for j in others:
                f_ag(it, q, j).wait_send()


def per_device(
    tile_values,
    tile_row,
    tile_column,
    unit_cost,
    capacity,
    demand,
    row_kind,
    primal_start,
    dual_start,
):
    dims = (SLOTS, RB, CB)
    hit = (tile_row[:, None, None] == lax.broadcasted_iota(jnp.int32, dims, 1)) & (
        tile_column[:, None, None] == lax.broadcasted_iota(jnp.int32, dims, 2)
    )
    inv = jnp.max(jnp.where(hit, lax.broadcasted_iota(jnp.int32, dims, 0), -1), axis=0)
    vmem = pl.BlockSpec(memory_space=pltpu.VMEM)
    f32, bf16 = jnp.float32, jnp.bfloat16
    dma = pltpu.SemaphoreType.DMA
    return pl.pallas_call(
        kernel,
        out_shape=(
            jax.ShapeDtypeStruct((CB, T, S), f32),
            jax.ShapeDtypeStruct((RB, T, S), f32),
        ),
        in_specs=[pl.BlockSpec(memory_space=pltpu.SMEM)]
        + [pl.BlockSpec(memory_space=pl.ANY)] * 7,
        out_specs=(vmem, vmem),
        scratch_shapes=[
            pltpu.VMEM((SLOTS, T, T), bf16),
            pltpu.VMEM((CB, T), f32),
            pltpu.VMEM((CB, T), f32),
            pltpu.VMEM((RB, T), jnp.int32),
            pltpu.VMEM((CB, T, S), f32),
            pltpu.VMEM((RB, T, S), f32),
            pltpu.VMEM((T, S), f32),
            pltpu.VMEM((RB * T, CB * T), bf16),
            pltpu.VMEM((ITERS + 1, CB, S, T), f32),
            pltpu.VMEM((ITERS + 1, RB, S, T), f32),
            pltpu.VMEM((S, RB * T), bf16),
            pltpu.VMEM((S, CB * T), bf16),
            pltpu.VMEM((ITERS, CB, S, T), f32),
            pltpu.VMEM((ITERS, NQ, CB, H, T), f32),
            pltpu.VMEM((ITERS, NQ, 2, 8, H, T), f32),
            pltpu.VMEM((ITERS, NQ, 2, 8, H, T), f32),
            pltpu.VMEM((ITERS, NQ, 2, 8, H, T), f32),
            pltpu.VMEM((ITERS, RB, S, T), f32),
            pltpu.VMEM((ITERS, NQ, len(PLANE), FR, T), f32),
            pltpu.VMEM((S, T), f32),
            dma((7,)),
            dma((ITERS, 4, NQ, 2, 8)),
            dma((ITERS, 4, NQ, 2, 8)),
            dma((ITERS, 2, NQ, 4)),
            dma((ITERS, 2, NQ, 4)),
            dma((ITERS, NQ, 2, len(PLANE))),
            dma((ITERS, NQ, 2, len(PLANE))),
        ],
        compiler_params=pltpu.CompilerParams(
            collective_id=0, has_side_effects=True, vmem_limit_bytes=56 << 20
        ),
        cost_estimate=pl.CostEstimate(
            flops=8 * SLOTS * T * T * S, bytes_accessed=6 << 20, transcendentals=0
        ),
    )(
        inv,
        tile_values,
        unit_cost,
        capacity,
        demand,
        row_kind,
        primal_start,
        dual_start,
    )


def solution(mesh):
    placed = (
        P(("col", "row"), None, None),
        P(("col", "row")),
        P(("col", "row")),
        P("col", None),
        P("col", None),
        P("row", None, None),
        P("row", None),
        P("col", None, None),
        P("row", None, None),
    )
    return jax.shard_map(
        per_device,
        mesh=mesh,
        in_specs=placed,
        out_specs=(P("col", None, None), P("row", None, None)),
        check_vma=False,
    )
```

```python
import jax
import jax.numpy as jnp
from jax import lax
from jax.experimental import pallas as pl
from jax.experimental.pallas import tpu as pltpu
from jax.sharding import PartitionSpec as P

ITERS = 2
NX, NY, NZ = 4, 4, 16
RB, CB, T, S = 8, 16, 128, 128
NQ = 2
SQ = S // NQ
H = SQ // 2
FR = SQ // 2
SLOTS = 48

PARENT = {1: 0, 3: 0, 6: 0, 2: 3, 4: 3, 5: 6, 7: 6, 8: 6}
HEADS = (6, 3, 1)
OFFS = (0, 1, -1, 3, -3, 6, -6, 2, -2, 4, -4, 5, -5, 7, -7, 8)
POS = {o: p for p, o in enumerate(OFFS)}
POS[-8] = POS[8]
PARTS = ((0, 7), (7, 11), (11, 16))
GROUPS = ((0, 1), (1, 7), (7, 11), (11, 16))
LEAVES = {1: (4, 2), 2: (8, 7, 5)}
HOPS = sorted({s * (d - u) for d, u in PARENT.items() for s in (1, -1)})

PLANE = sorted(
    [(a, b) for a in range(NX) for b in range(NY) if a or b],
    key=lambda o: -(min(o[0], NX - o[0]) + min(o[1], NY - o[1])),
)

primal_step = 0.5
dual_step = 0.5


def children(d):
    return [c for c, u in PARENT.items() if u == d]


def half(s, d):
    if d == 8:
        return (0 if s == 1 else H // 2), H // 2
    return 0, H


def kernel(
    inv_ref,
    tiles_hbm,
    cost_hbm,
    cap_hbm,
    demand_hbm,
    kind_hbm,
    primal_hbm,
    dual_hbm,
    primal_out,
    dual_out,
    tiles,
    cost,
    cap,
    kind,
    primal0,
    dual0,
    dem0,
    kd,
    pt,
    dt,
    dl,
    ext,
    ap,
    sib,
    rs_s,
    rs_r,
    fp,
    rx,
    dem,
    local_sem,
    ring_send,
    ring_recv,
    sib_send,
    sib_recv,
    f_send,
    f_recv,
):
    col = lax.axis_index("col")
    row = lax.axis_index("row")
    x, y = lax.div(col, NY), lax.rem(col, NY)
    z, core = lax.div(row, 2), lax.rem(row, 2)
    own_at = [pl.multiple_of(q * SQ + core * H, H) for q in range(NQ)]
    oth_at = [pl.multiple_of(q * SQ + (1 - core) * H, H) for q in range(NQ)]
    block_of = [lax.rem(z + OFFS[p] + NZ, NZ) for p in range(CB)]
    z_row = {d: lax.rem(z + d + NZ, NZ) * 2 + core for d in HOPS}
    sibling = (col, z * 2 + 1 - core)
    x_at = [lax.rem(x + d, NX) for d in range(NX)]
    y_at = [lax.rem(y + d, NY) for d in range(NY)]
    plane_at = {
        (a, b): x_at[a] * NY + y_at[b] for a in range(NX) for b in range(NY)
    }
    block_own = lax.div(col, 2)

    def own(q):
        return own_at[q]

    def oth(q):
        return oth_at[q]

    def block_at(p):
        return block_of[p]

    def zdev(d):
        return (col, z_row[d])

    loads = [
        pltpu.make_async_copy(src, dst, local_sem.at[n])
        for n, (src, dst) in enumerate(
            [
                (dual_hbm, dual0),
                (tiles_hbm, tiles),
                (primal_hbm, primal0),
                (cost_hbm, cost),
                (cap_hbm, cap),
                (kind_hbm, kind),
                (demand_hbm.at[block_own], dem0),
            ]
        )
    ]
    for load in loads:
        load.start()

    barrier = pltpu.get_barrier_semaphore()
    peers = [zdev(d) for d in HOPS] + [sibling]
    peers += [(plane_at[o], row) for o in PLANE]
    for peer in peers:
        pl.semaphore_signal(
            barrier, inc=1, device_id=peer, device_id_type=pl.DeviceIdType.MESH
        )

    def remote(src, dst, ss, rs, dev):
        return pltpu.make_async_remote_copy(
            src_ref=src,
            dst_ref=dst,
            send_sem=ss,
            recv_sem=rs,
            device_id=dev,
            device_id_type=pl.DeviceIdType.MESH,
        )

    def side(s):
        return 0 if s == 1 else 1

    def rs_copy(it, q, s, d):
        i = (it, q, side(s), d - 1, pl.ds(0, half(s, d)[1]))
        return remote(
            rs_s.at[i], rs_r.at[i], ring_send.at[it, 0, q, side(s), d - 1],
            ring_recv.at[it, 0, q, side(s), d - 1], zdev(s * (d - PARENT[d])),
        )

    def own_rows(q, s, d):
        start, size = half(s, d)
        return pl.ds(pl.multiple_of(own(q) + start, 16), size)

    def ag_copy(it, q, s, d):
        rows = own_rows(q, s, d)
        return remote(
            pt.at[it + 1, POS[-s * PARENT[d]], rows, :],
            pt.at[it + 1, POS[-s * d], rows, :],
            ring_send.at[it, 1, q, side(s), d - 1],
            ring_recv.at[it, 1, q, side(s), d - 1], zdev(s * (d - PARENT[d])),
        )

    def sib_rs(it, q, n):
        lo, hi = PARTS[n]
        return remote(
            ap.at[it, lo:hi, pl.ds(oth(q), H), :], sib.at[it, q, lo:hi],
            sib_send.at[it, 0, q, n], sib_recv.at[it, 0, q, n], sibling,
        )

    def sib_ag(it, q, n, rows):
        lo, hi = GROUPS[n]
        part = pt.at[it + 1, lo:hi, pl.ds(rows, H), :]
        return remote(
            part, part, sib_send.at[it, 1, q, n], sib_recv.at[it, 1, q, n], sibling
        )

    def chunk(q, k):
        return lax.div(k, 2), pl.ds(
            pl.multiple_of(q * SQ + lax.rem(k, 2) * FR, FR), FR
        )

    def back(o):
        return (NX - o[0]) % NX, (NY - o[1]) % NY

    def f_rs(it, q, j):
        k = plane_at[PLANE[j]]
        block, rows = chunk(q, k)
        return remote(
            fp.at[it, block, rows, :], rx.at[it, q, j],
            f_send.at[it, q, 0, j], f_recv.at[it, q, 0, j], (k, row),
        )

    def f_ag(it, q, j, arrival=False):
        block, rows = chunk(q, plane_at[back(PLANE[j])] if arrival else col)
        part = dt.at[it + 1, block, rows, :]
        return remote(
            part, part, f_send.at[it, q, 1, j], f_recv.at[it, q, 1, j],
            (plane_at[PLANE[j]], row),
        )

    others = range(len(PLANE))
    near_first = tuple(reversed(others))

    def build(lo, hi):
        def rows_of(r, _):
            r0 = pl.multiple_of(r * T, T)
            for p in range(lo, hi):
                idx = inv_ref[r * CB + block_at(p)]
                tile = tiles[jnp.maximum(idx, 0)]
                tile = jnp.where(idx >= 0, tile, jnp.zeros_like(tile))
                kd[pl.ds(r0, T), p * T : (p + 1) * T] = tile
            return 0

        lax.fori_loop(0, RB, rows_of, 0)

    def f_ag_wait(it, q):
        for j in near_first:
            f_ag(it, q, j, True).wait_recv()

    def slab(q):
        return (q * SQ, SQ)

    def iteration(it, _):
        def adjoint(lo, hi, rows):
            r0, many = rows
            for p in range(lo, hi, 2):
                w = min(2, hi - p)
                res = jnp.dot(
                    dl[r0 : r0 + many, :],
                    kd[:, p * T : (p + w) * T],
                    preferred_element_type=jnp.float32,
                )
                for k in range(w):
                    ap[it, p + k, r0 : r0 + many] = res[:, k * T : (k + 1) * T]

        def build_first(n):
            @pl.when(it == 0)
            def _():
                build(*PARTS[n])

        def rs_node(q, s, d):
            p = POS[s * d]
            start, size = half(s, d)
            value = (
                ap[it, p, own_rows(q, s, d), :] + sib[it, q, p, start : start + size, :]
            )
            for c in children(d):
                rs_copy(it, q, s, c).wait_recv()
                if c != 8:
                    value = value + rs_r[it, q, side(s), c - 1]
            rs_s[it, q, side(s), d - 1, :size] = value
            if 8 in children(d):
                at, many = half(s, 8)
                rows = slice(at, at + many)
                rs_s[it, q, side(s), d - 1, rows] = (
                    rs_s[it, q, side(s), d - 1, rows]
                    + rs_r[it, q, side(s), 7, :many]
                )
            rs_copy(it, q, s, d).start()

        def rs_part(n, q):
            sib_rs(it, q, n).wait_recv()
            for d in HEADS if n == 0 else LEAVES[n]:
                for s in (1, -1):
                    rs_node(q, s, d)

        @pl.when(it == 0)
        def _():
            loads[0].wait()
            for b in range(RB):
                dl[:, b * T : (b + 1) * T] = dual0[b].astype(jnp.bfloat16).T
            loads[1].wait()
            build(PARTS[1][0], PARTS[2][1])
            pl.semaphore_wait(barrier, len(peers))

        def partial(q, n):
            adjoint(*PARTS[n], slab(q))
            sib_rs(it, q, n).start()

        def begin(q):
            @pl.when(it > 0)
            def _():
                f_ag_wait(it - 1, q)
                r0, many = slab(q)
                for b in range(RB):
                    dl[r0 : r0 + many, b * T : (b + 1) * T] = dt[
                        it, b, r0 : r0 + many
                    ].astype(jnp.bfloat16)

            partial(q, 2)
            partial(q, 1)

        begin(0)
        build_first(0)
        partial(0, 0)
        rs_part(2, 0)
        rs_part(1, 0)
        begin(1)
        partial(1, 0)
        rs_part(2, 1)
        rs_part(1, 1)

        @pl.when(it == 0)
        def _():
            for load in loads[2:]:
                load.wait()
            for p in range(CB):
                pt[0, p] = primal0[block_at(p)].T
            for b in range(RB):
                dt[0, b] = dual0[b].T
            dem[...] = dem0[...].T

        for q in range(NQ):
            rs_part(0, q)

        for q in range(NQ):
            rows = pl.ds(own(q), H)
            total = ap[it, 0, rows, :] + sib[it, q, 0]
            for d in reversed(HEADS):
                for s in (1, -1):
                    rs_copy(it, q, s, d).wait_recv()
                    total = total + rs_r[it, q, side(s), d - 1]
            old = pt[it, 0, rows, :]
            pt[it + 1, 0, rows, :] = jnp.minimum(
                jnp.maximum(old - primal_step * (cost[pl.ds(z, 1), :] - total), 0.0),
                cap[pl.ds(z, 1), :],
            )
            for d in HEADS:
                for s in (1, -1):
                    ag_copy(it, q, s, d).start()
            sib_ag(it, q, 0, own(q)).start()

        def ag_heads(q):
            for d in HEADS:
                for s in (1, -1):
                    ag_copy(it, q, s, d).wait_recv()
                    for c in reversed(children(d)):
                        ag_copy(it, q, s, c).start()
            sib_ag(it, q, 1, own(q)).start()

        def ag_leaves(q):
            for n in (2, 1):
                for d in LEAVES[n]:
                    for s in (1, -1):
                        ag_copy(it, q, s, d).wait_recv()
                sib_ag(it, q, n + 1, own(q)).start()

        def forward(lo, hi, rows, first):
            r0, many = rows
            at = slice(r0, r0 + many)
            for p in range(lo, hi):
                ext[at, p * T : (p + 1) * T] = (
                    2.0 * pt[it + 1, p, at] - pt[it, p, at]
                ).astype(jnp.bfloat16)
            for n in range(0, RB, 2):
                res = lax.dot_general(
                    ext[at, lo * T : hi * T],
                    kd[n * T : (n + 2) * T, lo * T : hi * T],
                    (((1,), (1,)), ((), ())),
                    preferred_element_type=jnp.float32,
                )
                for k in range(2):
                    part = res[:, k * T : (k + 1) * T]
                    fp[it, n + k, at] = part if first else fp[it, n + k, at] + part

        def forward_heads(q):
            sib_ag(it, q, 0, oth(q)).wait_recv()
            sib_ag(it, q, 1, oth(q)).wait_recv()
            forward(0, 7, slab(q), True)

        def forward_leaves(q):
            sib_ag(it, q, 3, oth(q)).wait_recv()
            sib_ag(it, q, 2, oth(q)).wait_recv()
            forward(7, 16, slab(q), False)
            for j in others:
                f_rs(it, q, j).start()

        ag_heads(0)
        ag_heads(1)
        forward_heads(0)
        ag_leaves(0)
        forward_heads(1)
        forward_leaves(0)
        ag_leaves(1)
        forward_leaves(1)

        @pl.when(it == ITERS - 1)
        def _():
            for p in range(CB):
                primal_out[block_at(p)] = pt[ITERS, p].T

        for q in range(NQ):
            for s in (1, -1):
                for d in PARENT:
                    ag_copy(it, q, s, d).wait_send()
                    rs_copy(it, q, s, d).wait_send()
            for n in range(len(GROUPS)):
                sib_ag(it, q, n, own(q)).wait_send()
            for n in range(len(PARTS)):
                sib_rs(it, q, n).wait_send()

        for q in range(NQ):
            block, rows = chunk(q, col)
            forward_sum = fp[it, block, rows, :]
            for j in near_first:
                f_rs(it, q, j).wait_recv()
                forward_sum = forward_sum + rx[it, q, j]
            new = dt[it, block, rows, :] + dual_step * (dem[rows, :] - forward_sum)
            new = jnp.where(kind[pl.ds(block, 1), :] == 1, jnp.maximum(new, 0.0), new)
            dt[it + 1, block, rows, :] = new
            for j in others:
                f_ag(it, q, j).start()
        for q in range(NQ):
            for j in others:
                f_rs(it, q, j).wait_send()
        return 0

    lax.fori_loop(0, ITERS, iteration, 0)
    for q in range(NQ):
        f_ag_wait(ITERS - 1, q)
    for b in range(RB):
        dual_out[b] = dt[ITERS, b].T

    for it in range(ITERS):
        for q in range(NQ):
            for j in others:
                f_ag(it, q, j).wait_send()


def per_device(
    tile_values,
    tile_row,
    tile_column,
    unit_cost,
    capacity,
    demand,
    row_kind,
    primal_start,
    dual_start,
):
    place = jnp.where(tile_row < RB, tile_row * CB + tile_column, RB * CB)
    slot = jnp.arange(SLOTS, dtype=jnp.int32)
    hit = place[:, None] == jnp.arange(RB * CB, dtype=jnp.int32)[None, :]
    inv = jnp.max(jnp.where(hit, slot[:, None], -1), axis=0)
    vmem = pl.BlockSpec(memory_space=pltpu.VMEM)
    f32, bf16 = jnp.float32, jnp.bfloat16
    dma = pltpu.SemaphoreType.DMA
    return pl.pallas_call(
        kernel,
        out_shape=(
            jax.ShapeDtypeStruct((CB, T, S), f32),
            jax.ShapeDtypeStruct((RB, T, S), f32),
        ),
        in_specs=[pl.BlockSpec(memory_space=pltpu.SMEM)]
        + [pl.BlockSpec(memory_space=pl.ANY)] * 7,
        out_specs=(vmem, vmem),
        scratch_shapes=[
            pltpu.VMEM((SLOTS, T, T), bf16),
            pltpu.VMEM((CB, T), f32),
            pltpu.VMEM((CB, T), f32),
            pltpu.VMEM((RB, T), jnp.int32),
            pltpu.VMEM((CB, T, S), f32),
            pltpu.VMEM((RB, T, S), f32),
            pltpu.VMEM((T, S), f32),
            pltpu.VMEM((RB * T, CB * T), bf16),
            pltpu.VMEM((ITERS + 1, CB, S, T), f32),
            pltpu.VMEM((ITERS + 1, RB, S, T), f32),
            pltpu.VMEM((S, RB * T), bf16),
            pltpu.VMEM((S, CB * T), bf16),
            pltpu.VMEM((ITERS, CB, S, T), f32),
            pltpu.VMEM((ITERS, NQ, CB, H, T), f32),
            pltpu.VMEM((ITERS, NQ, 2, 8, H, T), f32),
            pltpu.VMEM((ITERS, NQ, 2, 8, H, T), f32),
            pltpu.VMEM((ITERS, RB, S, T), f32),
            pltpu.VMEM((ITERS, NQ, len(PLANE), FR, T), f32),
            pltpu.VMEM((S, T), f32),
            dma((7,)),
            dma((ITERS, 2, NQ, 2, 8)),
            dma((ITERS, 2, NQ, 2, 8)),
            dma((ITERS, 2, NQ, 4)),
            dma((ITERS, 2, NQ, 4)),
            dma((ITERS, NQ, 2, len(PLANE))),
            dma((ITERS, NQ, 2, len(PLANE))),
        ],
        compiler_params=pltpu.CompilerParams(
            collective_id=0, has_side_effects=True, vmem_limit_bytes=56 << 20
        ),
        cost_estimate=pl.CostEstimate(
            flops=8 * SLOTS * T * T * S, bytes_accessed=6 << 20, transcendentals=0
        ),
    )(
        inv,
        tile_values,
        unit_cost,
        capacity,
        demand,
        row_kind,
        primal_start,
        dual_start,
    )


def solution(mesh):
    placed = (
        P(("col", "row"), None, None),
        P(("col", "row")),
        P(("col", "row")),
        P("col", None),
        P("col", None),
        P("row", None, None),
        P("row", None),
        P("col", None, None),
        P("row", None, None),
    )
    return jax.shard_map(
        per_device,
        mesh=mesh,
        in_specs=placed,
        out_specs=(P("col", None, None), P("row", None, None)),
        check_vma=False,
    )
```

```python
import jax
import jax.numpy as jnp
from jax import lax
from jax.experimental import pallas as pl
from jax.experimental.pallas import tpu as pltpu
from jax.sharding import PartitionSpec as P

ITERS = 2
NX, NY, NZ = 4, 4, 16
RB, CB, T, S = 8, 16, 128, 128
NQ = 2
SQ = S // NQ
H = SQ // 2
FR = SQ // 2
SLOTS = 48

PARENT = {1: 0, 3: 0, 6: 0, 2: 3, 4: 3, 5: 6, 7: 6, 8: 6}
HEADS = (6, 3, 1)
OFFS = (0, 1, -1, 3, -3, 6, -6, 2, -2, 4, -4, 5, -5, 7, -7, 8)
POS = {o: p for p, o in enumerate(OFFS)}
POS[-8] = POS[8]
PARTS = ((0, 7), (7, 11), (11, 16))
GROUPS = ((0, 1), (1, 7), (7, 11), (11, 16))
LEAVES = {1: (4, 2), 2: (8, 7, 5)}
HOPS = sorted({s * (d - u) for d, u in PARENT.items() for s in (1, -1)})

PLANE = sorted(
    [(a, b) for a in range(NX) for b in range(NY) if a or b],
    key=lambda o: -(min(o[0], NX - o[0]) + min(o[1], NY - o[1])),
)

primal_step = 0.5
dual_step = 0.5


def children(d):
    return [c for c, u in PARENT.items() if u == d]


def half(s, d):
    if d == 8:
        return (0 if s == 1 else H // 2), H // 2
    return 0, H


def kernel(
    inv_ref,
    tiles_hbm,
    cost_hbm,
    cap_hbm,
    demand_hbm,
    kind_hbm,
    primal_hbm,
    dual_hbm,
    primal_out,
    dual_out,
    tiles,
    cost,
    cap,
    kind,
    primal0,
    dual0,
    dem0,
    kd,
    pt,
    dt,
    dl,
    ext,
    ap,
    sib,
    rs_s,
    rs_r,
    fp,
    rx,
    primal_t,
    dem,
    local_sem,
    leave_sem,
    ring_send,
    ring_recv,
    sib_send,
    sib_recv,
    f_send,
    f_recv,
):
    col = lax.axis_index("col")
    row = lax.axis_index("row")
    x, y = lax.div(col, NY), lax.rem(col, NY)
    z, core = lax.div(row, 2), lax.rem(row, 2)
    own_at = [pl.multiple_of(q * SQ + core * H, H) for q in range(NQ)]
    oth_at = [pl.multiple_of(q * SQ + (1 - core) * H, H) for q in range(NQ)]
    block_of = [lax.rem(z + OFFS[p] + NZ, NZ) for p in range(CB)]
    z_row = {d: lax.rem(z + d + NZ, NZ) * 2 + core for d in HOPS}
    sibling = (col, z * 2 + 1 - core)
    x_at = [lax.rem(x + d, NX) for d in range(NX)]
    y_at = [lax.rem(y + d, NY) for d in range(NY)]
    plane_at = {
        (a, b): x_at[a] * NY + y_at[b] for a in range(NX) for b in range(NY)
    }
    block_own = lax.div(col, 2)

    def own(q):
        return own_at[q]

    def oth(q):
        return oth_at[q]

    def block_at(p):
        return block_of[p]

    def zdev(d):
        return (col, z_row[d])

    loads = [
        pltpu.make_async_copy(src, dst, local_sem.at[n])
        for n, (src, dst) in enumerate(
            [
                (dual_hbm, dual0),
                (tiles_hbm, tiles),
                (primal_hbm, primal0),
                (cost_hbm, cost),
                (cap_hbm, cap),
                (kind_hbm, kind),
                (demand_hbm.at[block_own], dem0),
            ]
        )
    ]
    for load in loads:
        load.start()

    barrier = pltpu.get_barrier_semaphore()
    peers = [zdev(d) for d in HOPS] + [sibling]
    peers += [(plane_at[o], row) for o in PLANE]
    for peer in peers:
        pl.semaphore_signal(
            barrier, inc=1, device_id=peer, device_id_type=pl.DeviceIdType.MESH
        )

    def remote(src, dst, ss, rs, dev):
        return pltpu.make_async_remote_copy(
            src_ref=src,
            dst_ref=dst,
            send_sem=ss,
            recv_sem=rs,
            device_id=dev,
            device_id_type=pl.DeviceIdType.MESH,
        )

    def side(s):
        return 0 if s == 1 else 1

    def rs_copy(it, q, s, d):
        i = (it, q, side(s), d - 1, pl.ds(0, half(s, d)[1]))
        return remote(
            rs_s.at[i], rs_r.at[i], ring_send.at[it, 0, q, side(s), d - 1],
            ring_recv.at[it, 0, q, side(s), d - 1], zdev(s * (d - PARENT[d])),
        )

    def own_rows(q, s, d):
        start, size = half(s, d)
        return pl.ds(pl.multiple_of(own(q) + start, 16), size)

    def ag_copy(it, q, s, d):
        rows = own_rows(q, s, d)
        return remote(
            pt.at[it + 1, POS[-s * PARENT[d]], rows, :],
            pt.at[it + 1, POS[-s * d], rows, :],
            ring_send.at[it, 1, q, side(s), d - 1],
            ring_recv.at[it, 1, q, side(s), d - 1], zdev(s * (d - PARENT[d])),
        )

    def sib_rs(it, q, n):
        lo, hi = PARTS[n]
        return remote(
            ap.at[it, lo:hi, pl.ds(oth(q), H), :], sib.at[it, q, lo:hi],
            sib_send.at[it, 0, q, n], sib_recv.at[it, 0, q, n], sibling,
        )

    def sib_ag(it, q, n, rows):
        lo, hi = GROUPS[n]
        part = pt.at[it + 1, lo:hi, pl.ds(rows, H), :]
        return remote(
            part, part, sib_send.at[it, 1, q, n], sib_recv.at[it, 1, q, n], sibling
        )

    def chunk(q, k):
        return lax.div(k, 2), pl.ds(
            pl.multiple_of(q * SQ + lax.rem(k, 2) * FR, FR), FR
        )

    def back(o):
        return (NX - o[0]) % NX, (NY - o[1]) % NY

    def f_rs(it, q, j):
        k = plane_at[PLANE[j]]
        block, rows = chunk(q, k)
        return remote(
            fp.at[it, block, rows, :], rx.at[it, q, j],
            f_send.at[it, q, 0, j], f_recv.at[it, q, 0, j], (k, row),
        )

    def f_ag(it, q, j, arrival=False):
        block, rows = chunk(q, plane_at[back(PLANE[j])] if arrival else col)
        part = dt.at[it + 1, block, rows, :]
        return remote(
            part, part, f_send.at[it, q, 1, j], f_recv.at[it, q, 1, j],
            (plane_at[PLANE[j]], row),
        )

    others = range(len(PLANE))
    near_first = tuple(reversed(others))

    def build(lo, hi):
        def rows_of(r, _):
            r0 = pl.multiple_of(r * T, T)
            for p in range(lo, hi):
                idx = inv_ref[r * CB + block_at(p)]
                tile = tiles[jnp.maximum(idx, 0)]
                tile = jnp.where(idx >= 0, tile, jnp.zeros_like(tile))
                kd[pl.ds(r0, T), p * T : (p + 1) * T] = tile
            return 0

        lax.fori_loop(0, RB, rows_of, 0)

    def f_ag_wait(it, q):
        for j in near_first:
            f_ag(it, q, j, True).wait_recv()

    def leave(p):
        return pltpu.make_async_copy(
            primal_t.at[p], primal_out.at[block_at(p)], leave_sem.at[p]
        )

    def slab(q):
        return (q * SQ, SQ)

    def iteration(it, _):
        def adjoint(lo, hi, rows):
            r0, many = rows
            for p in range(lo, hi, 2):
                w = min(2, hi - p)
                res = jnp.dot(
                    dl[r0 : r0 + many, :],
                    kd[:, p * T : (p + w) * T],
                    preferred_element_type=jnp.float32,
                )
                for k in range(w):
                    ap[it, p + k, r0 : r0 + many] = res[:, k * T : (k + 1) * T]

        def build_first(n):
            @pl.when(it == 0)
            def _():
                build(*PARTS[n])

        def rs_node(q, s, d):
            p = POS[s * d]
            start, size = half(s, d)
            value = (
                ap[it, p, own_rows(q, s, d), :] + sib[it, q, p, start : start + size, :]
            )
            for c in children(d):
                rs_copy(it, q, s, c).wait_recv()
                if c != 8:
                    value = value + rs_r[it, q, side(s), c - 1]
            rs_s[it, q, side(s), d - 1, :size] = value
            if 8 in children(d):
                at, many = half(s, 8)
                rows = slice(at, at + many)
                rs_s[it, q, side(s), d - 1, rows] = (
                    rs_s[it, q, side(s), d - 1, rows]
                    + rs_r[it, q, side(s), 7, :many]
                )
            rs_copy(it, q, s, d).start()

        def rs_part(n, q):
            sib_rs(it, q, n).wait_recv()
            for d in HEADS if n == 0 else LEAVES[n]:
                for s in (1, -1):
                    rs_node(q, s, d)

        @pl.when(it == 0)
        def _():
            loads[0].wait()
            for b in range(RB):
                dl[:, b * T : (b + 1) * T] = dual0[b].astype(jnp.bfloat16).T
            loads[1].wait()
            build(PARTS[1][0], PARTS[2][1])
            pl.semaphore_wait(barrier, len(peers))

        def partial(q, n):
            adjoint(*PARTS[n], slab(q))
            sib_rs(it, q, n).start()

        def begin(q):
            @pl.when(it > 0)
            def _():
                f_ag_wait(it - 1, q)
                r0, many = slab(q)
                for b in range(RB):
                    dl[r0 : r0 + many, b * T : (b + 1) * T] = dt[
                        it, b, r0 : r0 + many
                    ].astype(jnp.bfloat16)

            partial(q, 2)
            partial(q, 1)

        begin(0)
        build_first(0)
        partial(0, 0)
        rs_part(2, 0)
        rs_part(1, 0)
        begin(1)
        partial(1, 0)
        rs_part(2, 1)
        rs_part(1, 1)

        @pl.when(it == 0)
        def _():
            for load in loads[2:]:
                load.wait()
            pt[0, 0] = primal0[block_at(0)].T

        for q in range(NQ):
            rs_part(0, q)

        for q in range(NQ):
            rows = pl.ds(own(q), H)
            total = ap[it, 0, rows, :] + sib[it, q, 0]
            for d in reversed(HEADS):
                for s in (1, -1):
                    rs_copy(it, q, s, d).wait_recv()
                    total = total + rs_r[it, q, side(s), d - 1]
            old = pt[it, 0, rows, :]
            pt[it + 1, 0, rows, :] = jnp.minimum(
                jnp.maximum(old - primal_step * (cost[pl.ds(z, 1), :] - total), 0.0),
                cap[pl.ds(z, 1), :],
            )
            for d in HEADS:
                for s in (1, -1):
                    ag_copy(it, q, s, d).start()
            sib_ag(it, q, 0, own(q)).start()

        @pl.when(it == 0)
        def _():
            for p in range(1, CB):
                pt[0, p] = primal0[block_at(p)].T
            for b in range(RB):
                dt[0, b] = dual0[b].T
            dem[...] = dem0[...].T

        def ag_heads(q):
            for d in HEADS:
                for s in (1, -1):
                    ag_copy(it, q, s, d).wait_recv()
                    for c in reversed(children(d)):
                        ag_copy(it, q, s, c).start()
            sib_ag(it, q, 1, own(q)).start()

        def ag_leaves(q):
            for n in (2, 1):
                for d in LEAVES[n]:
                    for s in (1, -1):
                        ag_copy(it, q, s, d).wait_recv()
                sib_ag(it, q, n + 1, own(q)).start()

        def forward(lo, hi, rows, first):
            r0, many = rows
            at = slice(r0, r0 + many)
            for p in range(lo, hi):
                ext[at, p * T : (p + 1) * T] = (
                    2.0 * pt[it + 1, p, at] - pt[it, p, at]
                ).astype(jnp.bfloat16)
            for n in range(0, RB, 2):
                res = lax.dot_general(
                    ext[at, lo * T : hi * T],
                    kd[n * T : (n + 2) * T, lo * T : hi * T],
                    (((1,), (1,)), ((), ())),
                    preferred_element_type=jnp.float32,
                )
                for k in range(2):
                    part = res[:, k * T : (k + 1) * T]
                    fp[it, n + k, at] = part if first else fp[it, n + k, at] + part

        def forward_heads(q):
            sib_ag(it, q, 0, oth(q)).wait_recv()
            sib_ag(it, q, 1, oth(q)).wait_recv()
            forward(0, 7, slab(q), True)

        def forward_leaves(q):
            sib_ag(it, q, 3, oth(q)).wait_recv()
            sib_ag(it, q, 2, oth(q)).wait_recv()
            forward(7, 16, slab(q), False)
            for j in others:
                f_rs(it, q, j).start()

        ag_heads(0)
        ag_heads(1)
        forward_heads(0)
        ag_leaves(0)
        forward_heads(1)
        forward_leaves(0)
        ag_leaves(1)
        forward_leaves(1)

        @pl.when(it == ITERS - 1)
        def _():
            for p in range(CB):
                primal_t[p] = pt[ITERS, p].T
                leave(p).start()

        for q in range(NQ):
            for s in (1, -1):
                for d in PARENT:
                    ag_copy(it, q, s, d).wait_send()
                    rs_copy(it, q, s, d).wait_send()
            for n in range(len(GROUPS)):
                sib_ag(it, q, n, own(q)).wait_send()
            for n in range(len(PARTS)):
                sib_rs(it, q, n).wait_send()

        for q in range(NQ):
            block, rows = chunk(q, col)
            forward_sum = fp[it, block, rows, :]
            for j in near_first:
                f_rs(it, q, j).wait_recv()
                forward_sum = forward_sum + rx[it, q, j]
            new = dt[it, block, rows, :] + dual_step * (dem[rows, :] - forward_sum)
            new = jnp.where(kind[pl.ds(block, 1), :] == 1, jnp.maximum(new, 0.0), new)
            dt[it + 1, block, rows, :] = new
            for j in others:
                f_ag(it, q, j).start()
        for q in range(NQ):
            for j in others:
                f_rs(it, q, j).wait_send()
        return 0

    lax.fori_loop(0, ITERS, iteration, 0)
    for q in range(NQ):
        f_ag_wait(ITERS - 1, q)
    for b in range(RB):
        dual_out[b] = dt[ITERS, b].T
    for p in range(CB):
        leave(p).wait()

    for it in range(ITERS):
        for q in range(NQ):
            for j in others:
                f_ag(it, q, j).wait_send()


def hand_over(primal, dual, primal_out, dual_out, sem):
    copies = []
    for src, dst, blocks in ((primal, primal_out, CB), (dual, dual_out, RB)):
        for b in range(0, blocks, 4):
            copies.append(
                pltpu.make_async_copy(
                    src.at[b : b + 4], dst.at[b : b + 4], sem.at[len(copies)]
                )
            )
    for copy in copies:
        copy.start()
    for copy in copies:
        copy.wait()


def per_device(
    tile_values,
    tile_row,
    tile_column,
    unit_cost,
    capacity,
    demand,
    row_kind,
    primal_start,
    dual_start,
):
    place = jnp.where(tile_row < RB, tile_row * CB + tile_column, RB * CB)
    slot = jnp.arange(SLOTS, dtype=jnp.int32)
    hit = place[:, None] == jnp.arange(RB * CB, dtype=jnp.int32)[None, :]
    inv = jnp.max(jnp.where(hit, slot[:, None], -1), axis=0)
    vmem = pl.BlockSpec(memory_space=pltpu.VMEM)
    hbm = pl.BlockSpec(memory_space=pl.ANY)
    f32, bf16 = jnp.float32, jnp.bfloat16
    dma = pltpu.SemaphoreType.DMA
    outs = (
        jax.ShapeDtypeStruct((CB, T, S), f32),
        jax.ShapeDtypeStruct((RB, T, S), f32),
    )
    results = pl.pallas_call(
        kernel,
        out_shape=outs,
        in_specs=[pl.BlockSpec(memory_space=pltpu.SMEM)]
        + [hbm] * 7,
        out_specs=(hbm, vmem),
        scratch_shapes=[
            pltpu.VMEM((SLOTS, T, T), bf16),
            pltpu.VMEM((CB, T), f32),
            pltpu.VMEM((CB, T), f32),
            pltpu.VMEM((RB, T), jnp.int32),
            pltpu.VMEM((CB, T, S), f32),
            pltpu.VMEM((RB, T, S), f32),
            pltpu.VMEM((T, S), f32),
            pltpu.VMEM((RB * T, CB * T), bf16),
            pltpu.VMEM((ITERS + 1, CB, S, T), f32),
            pltpu.VMEM((ITERS + 1, RB, S, T), f32),
            pltpu.VMEM((S, RB * T), bf16),
            pltpu.VMEM((S, CB * T), bf16),
            pltpu.VMEM((ITERS, CB, S, T), f32),
            pltpu.VMEM((ITERS, NQ, CB, H, T), f32),
            pltpu.VMEM((ITERS, NQ, 2, 8, H, T), f32),
            pltpu.VMEM((ITERS, NQ, 2, 8, H, T), f32),
            pltpu.VMEM((ITERS, RB, S, T), f32),
            pltpu.VMEM((ITERS, NQ, len(PLANE), FR, T), f32),
            pltpu.VMEM((CB, T, S), f32),
            pltpu.VMEM((S, T), f32),
            dma((7,)),
            dma((CB,)),
            dma((ITERS, 2, NQ, 2, 8)),
            dma((ITERS, 2, NQ, 2, 8)),
            dma((ITERS, 2, NQ, 4)),
            dma((ITERS, 2, NQ, 4)),
            dma((ITERS, NQ, 2, len(PLANE))),
            dma((ITERS, NQ, 2, len(PLANE))),
        ],
        compiler_params=pltpu.CompilerParams(
            collective_id=0, has_side_effects=True, vmem_limit_bytes=56 << 20
        ),
        cost_estimate=pl.CostEstimate(
            flops=8 * SLOTS * T * T * S, bytes_accessed=6 << 20, transcendentals=0
        ),
    )(
        inv,
        tile_values,
        unit_cost,
        capacity,
        demand,
        row_kind,
        primal_start,
        dual_start,
    )
    return pl.pallas_call(
        hand_over,
        out_shape=outs,
        in_specs=[hbm] * 2,
        out_specs=(hbm, hbm),
        scratch_shapes=[dma((CB // 4 + RB // 4,))],
        compiler_params=pltpu.CompilerParams(vmem_limit_bytes=56 << 20),
    )(*results)


def solution(mesh):
    placed = (
        P(("col", "row"), None, None),
        P(("col", "row")),
        P(("col", "row")),
        P("col", None),
        P("col", None),
        P("row", None, None),
        P("row", None),
        P("col", None, None),
        P("row", None, None),
    )
    return jax.shard_map(
        per_device,
        mesh=mesh,
        in_specs=placed,
        out_specs=(P("col", None, None), P("row", None, None)),
        check_vma=False,
    )
```

```python
import jax
import jax.numpy as jnp
from jax import lax
from jax.experimental import pallas as pl
from jax.experimental.pallas import tpu as pltpu
from jax.sharding import PartitionSpec as P

ITERS = 2
NX, NY, NZ = 4, 4, 16
RB, CB, T, S = 8, 16, 128, 128
NQ = 2
SQ = S // NQ
H = SQ // 2
FR = SQ // 2
SLOTS = 48

PARENT = {1: 0, 3: 0, 6: 0, 2: 3, 4: 3, 5: 6, 7: 6, 8: 6}
HEADS = (6, 3, 1)
OFFS = (0, 1, -1, 3, -3, 6, -6, 2, -2, 4, -4, 5, -5, 7, -7, 8)
POS = {o: p for p, o in enumerate(OFFS)}
POS[-8] = POS[8]
PARTS = ((0, 7), (7, 11), (11, 16))
GROUPS = ((0, 1), (1, 7), (7, 11), (11, 16))
LEAVES = {1: (4, 2), 2: (8, 7, 5)}
HOPS = sorted({s * (d - u) for d, u in PARENT.items() for s in (1, -1)})

PLANE = sorted(
    [(a, b) for a in range(NX) for b in range(NY) if a or b],
    key=lambda o: -(min(o[0], NX - o[0]) + min(o[1], NY - o[1])),
)

primal_step = 0.5
dual_step = 0.5


def children(d):
    return [c for c, u in PARENT.items() if u == d]


def half(s, d):
    if d == 8:
        return (0 if s == 1 else H // 2), H // 2
    return 0, H


def kernel(
    inv_ref,
    tiles_hbm,
    cost_hbm,
    cap_hbm,
    demand_hbm,
    kind_hbm,
    primal_hbm,
    dual_hbm,
    primal_out,
    dual_out,
    tiles,
    cost,
    cap,
    kind,
    primal0,
    dual0,
    dem0,
    kd,
    pt,
    dt,
    dl,
    ext,
    ap,
    sib,
    rs_s,
    rs_r,
    fp,
    rx,
    primal_t,
    dem,
    local_sem,
    leave_sem,
    ring_send,
    ring_recv,
    sib_send,
    sib_recv,
    f_send,
    f_recv,
):
    col = lax.axis_index("col")
    row = lax.axis_index("row")
    x, y = lax.div(col, NY), lax.rem(col, NY)
    z, core = lax.div(row, 2), lax.rem(row, 2)
    own_at = [pl.multiple_of(q * SQ + core * H, H) for q in range(NQ)]
    oth_at = [pl.multiple_of(q * SQ + (1 - core) * H, H) for q in range(NQ)]
    block_of = [lax.rem(z + OFFS[p] + NZ, NZ) for p in range(CB)]
    z_row = {d: lax.rem(z + d + NZ, NZ) * 2 + core for d in HOPS}
    sibling = (col, z * 2 + 1 - core)
    x_at = [lax.rem(x + d, NX) for d in range(NX)]
    y_at = [lax.rem(y + d, NY) for d in range(NY)]
    plane_at = {
        (a, b): x_at[a] * NY + y_at[b] for a in range(NX) for b in range(NY)
    }
    block_own = lax.div(col, 2)

    def own(q):
        return own_at[q]

    def oth(q):
        return oth_at[q]

    def block_at(p):
        return block_of[p]

    def zdev(d):
        return (col, z_row[d])

    loads = [
        pltpu.make_async_copy(src, dst, local_sem.at[n])
        for n, (src, dst) in enumerate(
            [
                (dual_hbm, dual0),
                (tiles_hbm, tiles),
                (primal_hbm, primal0),
                (cost_hbm, cost),
                (cap_hbm, cap),
                (kind_hbm, kind),
                (demand_hbm.at[block_own], dem0),
            ]
        )
    ]
    for load in loads:
        load.start()

    barrier = pltpu.get_barrier_semaphore()
    peers = [zdev(d) for d in HOPS] + [sibling]
    peers += [(plane_at[o], row) for o in PLANE]
    for peer in peers:
        pl.semaphore_signal(
            barrier, inc=1, device_id=peer, device_id_type=pl.DeviceIdType.MESH
        )

    def remote(src, dst, ss, rs, dev):
        return pltpu.make_async_remote_copy(
            src_ref=src,
            dst_ref=dst,
            send_sem=ss,
            recv_sem=rs,
            device_id=dev,
            device_id_type=pl.DeviceIdType.MESH,
        )

    def side(s):
        return 0 if s == 1 else 1

    def rs_copy(it, q, s, d):
        i = (it, q, side(s), d - 1, pl.ds(0, half(s, d)[1]))
        return remote(
            rs_s.at[i], rs_r.at[i], ring_send.at[it, 0, q, side(s), d - 1],
            ring_recv.at[it, 0, q, side(s), d - 1], zdev(s * (d - PARENT[d])),
        )

    def own_rows(q, s, d):
        start, size = half(s, d)
        return pl.ds(pl.multiple_of(own(q) + start, 16), size)

    def ag_copy(it, q, s, d):
        rows = own_rows(q, s, d)
        return remote(
            pt.at[it + 1, POS[-s * PARENT[d]], rows, :],
            pt.at[it + 1, POS[-s * d], rows, :],
            ring_send.at[it, 1, q, side(s), d - 1],
            ring_recv.at[it, 1, q, side(s), d - 1], zdev(s * (d - PARENT[d])),
        )

    def sib_rs(it, q, n):
        lo, hi = PARTS[n]
        return remote(
            ap.at[it, lo:hi, pl.ds(oth(q), H), :], sib.at[it, q, lo:hi],
            sib_send.at[it, 0, q, n], sib_recv.at[it, 0, q, n], sibling,
        )

    def sib_ag(it, q, n, rows):
        lo, hi = GROUPS[n]
        part = pt.at[it + 1, lo:hi, pl.ds(rows, H), :]
        return remote(
            part, part, sib_send.at[it, 1, q, n], sib_recv.at[it, 1, q, n], sibling
        )

    def chunk(q, k):
        return lax.div(k, 2), pl.ds(
            pl.multiple_of(q * SQ + lax.rem(k, 2) * FR, FR), FR
        )

    def back(o):
        return (NX - o[0]) % NX, (NY - o[1]) % NY

    def f_rs(it, q, j):
        k = plane_at[PLANE[j]]
        block, rows = chunk(q, k)
        return remote(
            fp.at[it, block, rows, :], rx.at[it, q, j],
            f_send.at[it, q, 0, j], f_recv.at[it, q, 0, j], (k, row),
        )

    def f_ag(it, q, j, arrival=False):
        block, rows = chunk(q, plane_at[back(PLANE[j])] if arrival else col)
        part = dt.at[it + 1, block, rows, :]
        return remote(
            part, part, f_send.at[it, q, 1, j], f_recv.at[it, q, 1, j],
            (plane_at[PLANE[j]], row),
        )

    others = range(len(PLANE))
    near_first = tuple(reversed(others))

    def build(lo, hi):
        def rows_of(r, _):
            r0 = pl.multiple_of(r * T, T)
            for p in range(lo, hi):
                idx = inv_ref[r * CB + block_at(p)]
                tile = tiles[jnp.maximum(idx, 0)]
                tile = jnp.where(idx >= 0, tile, jnp.zeros_like(tile))
                kd[pl.ds(r0, T), p * T : (p + 1) * T] = tile
            return 0

        lax.fori_loop(0, RB, rows_of, 0)

    def f_ag_wait(it, q):
        for j in near_first:
            f_ag(it, q, j, True).wait_recv()

    def leave(p):
        return pltpu.make_async_copy(
            primal_t.at[p], primal_out.at[block_at(p)], leave_sem.at[p]
        )

    def slab(q):
        return (q * SQ, SQ)

    def iteration(it, _):
        def adjoint(lo, hi, rows):
            r0, many = rows
            for p in range(lo, hi, 2):
                w = min(2, hi - p)
                res = jnp.dot(
                    dl[r0 : r0 + many, :],
                    kd[:, p * T : (p + w) * T],
                    preferred_element_type=jnp.float32,
                )
                for k in range(w):
                    ap[it, p + k, r0 : r0 + many] = res[:, k * T : (k + 1) * T]

        def build_first(n):
            @pl.when(it == 0)
            def _():
                build(*PARTS[n])

        def rs_node(q, s, d):
            p = POS[s * d]
            start, size = half(s, d)
            value = (
                ap[it, p, own_rows(q, s, d), :] + sib[it, q, p, start : start + size, :]
            )
            for c in children(d):
                rs_copy(it, q, s, c).wait_recv()
                if c != 8:
                    value = value + rs_r[it, q, side(s), c - 1]
            rs_s[it, q, side(s), d - 1, :size] = value
            if 8 in children(d):
                at, many = half(s, 8)
                rows = slice(at, at + many)
                rs_s[it, q, side(s), d - 1, rows] = (
                    rs_s[it, q, side(s), d - 1, rows]
                    + rs_r[it, q, side(s), 7, :many]
                )
            rs_copy(it, q, s, d).start()

        def rs_part(n, q):
            sib_rs(it, q, n).wait_recv()
            for d in HEADS if n == 0 else LEAVES[n]:
                for s in (1, -1):
                    rs_node(q, s, d)

        @pl.when(it == 0)
        def _():
            loads[0].wait()
            for b in range(RB):
                dl[:, b * T : (b + 1) * T] = dual0[b].astype(jnp.bfloat16).T
            loads[1].wait()
            build(PARTS[1][0], PARTS[2][1])
            pl.semaphore_wait(barrier, len(peers))

        def partial(q, n):
            adjoint(*PARTS[n], slab(q))
            sib_rs(it, q, n).start()

        def begin(q):
            @pl.when(it > 0)
            def _():
                f_ag_wait(it - 1, q)
                r0, many = slab(q)
                for b in range(RB):
                    dl[r0 : r0 + many, b * T : (b + 1) * T] = dt[
                        it, b, r0 : r0 + many
                    ].astype(jnp.bfloat16)

            partial(q, 2)
            partial(q, 1)

        begin(0)
        build_first(0)
        partial(0, 0)
        rs_part(2, 0)
        rs_part(1, 0)
        begin(1)
        partial(1, 0)
        rs_part(2, 1)
        rs_part(1, 1)

        @pl.when(it == 0)
        def _():
            for load in loads[2:]:
                load.wait()
            pt[0, 0] = primal0[block_at(0)].T

        for q in range(NQ):
            rs_part(0, q)

        for q in range(NQ):
            rows = pl.ds(own(q), H)
            total = ap[it, 0, rows, :] + sib[it, q, 0]
            for d in reversed(HEADS):
                for s in (1, -1):
                    rs_copy(it, q, s, d).wait_recv()
                    total = total + rs_r[it, q, side(s), d - 1]
            old = pt[it, 0, rows, :]
            pt[it + 1, 0, rows, :] = jnp.minimum(
                jnp.maximum(old - primal_step * (cost[pl.ds(z, 1), :] - total), 0.0),
                cap[pl.ds(z, 1), :],
            )
            for d in HEADS:
                for s in (1, -1):
                    ag_copy(it, q, s, d).start()
            sib_ag(it, q, 0, own(q)).start()

        @pl.when(it == 0)
        def _():
            for p in range(1, CB):
                pt[0, p] = primal0[block_at(p)].T
            for b in range(RB):
                dt[0, b] = dual0[b].T
            dem[...] = dem0[...].T

        def ag_heads(q):
            for d in HEADS:
                for s in (1, -1):
                    ag_copy(it, q, s, d).wait_recv()
                    for c in reversed(children(d)):
                        ag_copy(it, q, s, c).start()
            sib_ag(it, q, 1, own(q)).start()

        def ag_leaves(q):
            for n in (2, 1):
                for d in LEAVES[n]:
                    for s in (1, -1):
                        ag_copy(it, q, s, d).wait_recv()
                sib_ag(it, q, n + 1, own(q)).start()

        def forward(lo, hi, rows, first):
            r0, many = rows
            at = slice(r0, r0 + many)
            for p in range(lo, hi):
                ext[at, p * T : (p + 1) * T] = (
                    2.0 * pt[it + 1, p, at] - pt[it, p, at]
                ).astype(jnp.bfloat16)
            for n in range(0, RB, 2):
                res = lax.dot_general(
                    ext[at, lo * T : hi * T],
                    kd[n * T : (n + 2) * T, lo * T : hi * T],
                    (((1,), (1,)), ((), ())),
                    preferred_element_type=jnp.float32,
                )
                for k in range(2):
                    part = res[:, k * T : (k + 1) * T]
                    fp[it, n + k, at] = part if first else fp[it, n + k, at] + part

        def forward_heads(q):
            sib_ag(it, q, 0, oth(q)).wait_recv()
            sib_ag(it, q, 1, oth(q)).wait_recv()
            forward(0, 7, slab(q), True)

        def forward_leaves(q):
            sib_ag(it, q, 3, oth(q)).wait_recv()
            sib_ag(it, q, 2, oth(q)).wait_recv()
            forward(7, 16, slab(q), False)
            for j in others:
                f_rs(it, q, j).start()

        ag_heads(0)
        ag_heads(1)
        forward_heads(0)
        ag_leaves(0)
        forward_heads(1)
        forward_leaves(0)
        ag_leaves(1)
        forward_leaves(1)

        @pl.when(it == ITERS - 1)
        def _():
            for p in range(CB):
                primal_t[p] = pt[ITERS, p].T
                leave(p).start()

        for q in range(NQ):
            for s in (1, -1):
                for d in PARENT:
                    ag_copy(it, q, s, d).wait_send()
                    rs_copy(it, q, s, d).wait_send()
            for n in range(len(GROUPS)):
                sib_ag(it, q, n, own(q)).wait_send()
            for n in range(len(PARTS)):
                sib_rs(it, q, n).wait_send()

        for q in range(NQ):
            block, rows = chunk(q, col)
            forward_sum = fp[it, block, rows, :]
            for j in near_first:
                f_rs(it, q, j).wait_recv()
                forward_sum = forward_sum + rx[it, q, j]
            new = dt[it, block, rows, :] + dual_step * (dem[rows, :] - forward_sum)
            new = jnp.where(kind[pl.ds(block, 1), :] == 1, jnp.maximum(new, 0.0), new)
            dt[it + 1, block, rows, :] = new
            for j in others:
                f_ag(it, q, j).start()
        for q in range(NQ):
            for j in others:
                f_rs(it, q, j).wait_send()
        return 0

    lax.fori_loop(0, ITERS, iteration, 0)
    for q in range(NQ):
        f_ag_wait(ITERS - 1, q)
    for b in range(RB):
        dual_out[b] = dt[ITERS, b].T
    for p in range(CB):
        leave(p).wait()

    for it in range(ITERS):
        for q in range(NQ):
            for j in others:
                f_ag(it, q, j).wait_send()


def hand_over(primal, dual, primal_out, dual_out, primal_v, dual_v, in_sem, out_sem):
    arrive, leave = [], []
    for src, mid, dst, blocks in (
        (primal, primal_v, primal_out, CB),
        (dual, dual_v, dual_out, RB),
    ):
        for b in range(0, blocks, 4):
            n, part = len(arrive), slice(b, b + 4)
            arrive.append(
                pltpu.make_async_copy(src.at[part], mid.at[part], in_sem.at[n])
            )
            leave.append(
                pltpu.make_async_copy(mid.at[part], dst.at[part], out_sem.at[n])
            )
    for copy in arrive:
        copy.start()
    for come, go in zip(arrive, leave):
        come.wait()
        go.start()
    for copy in leave:
        copy.wait()


def per_device(
    tile_values,
    tile_row,
    tile_column,
    unit_cost,
    capacity,
    demand,
    row_kind,
    primal_start,
    dual_start,
):
    place = jnp.where(tile_row < RB, tile_row * CB + tile_column, RB * CB)
    slot = jnp.arange(SLOTS, dtype=jnp.int32)
    hit = place[:, None] == jnp.arange(RB * CB, dtype=jnp.int32)[None, :]
    inv = jnp.max(jnp.where(hit, slot[:, None], -1), axis=0)
    vmem = pl.BlockSpec(memory_space=pltpu.VMEM)
    hbm = pl.BlockSpec(memory_space=pl.ANY)
    f32, bf16 = jnp.float32, jnp.bfloat16
    dma = pltpu.SemaphoreType.DMA
    outs = (
        jax.ShapeDtypeStruct((CB, T, S), f32),
        jax.ShapeDtypeStruct((RB, T, S), f32),
    )
    results = pl.pallas_call(
        kernel,
        out_shape=outs,
        in_specs=[pl.BlockSpec(memory_space=pltpu.SMEM)]
        + [hbm] * 7,
        out_specs=(hbm, vmem),
        scratch_shapes=[
            pltpu.VMEM((SLOTS, T, T), bf16),
            pltpu.VMEM((CB, T), f32),
            pltpu.VMEM((CB, T), f32),
            pltpu.VMEM((RB, T), jnp.int32),
            pltpu.VMEM((CB, T, S), f32),
            pltpu.VMEM((RB, T, S), f32),
            pltpu.VMEM((T, S), f32),
            pltpu.VMEM((RB * T, CB * T), bf16),
            pltpu.VMEM((ITERS + 1, CB, S, T), f32),
            pltpu.VMEM((ITERS + 1, RB, S, T), f32),
            pltpu.VMEM((S, RB * T), bf16),
            pltpu.VMEM((S, CB * T), bf16),
            pltpu.VMEM((ITERS, CB, S, T), f32),
            pltpu.VMEM((ITERS, NQ, CB, H, T), f32),
            pltpu.VMEM((ITERS, NQ, 2, 8, H, T), f32),
            pltpu.VMEM((ITERS, NQ, 2, 8, H, T), f32),
            pltpu.VMEM((ITERS, RB, S, T), f32),
            pltpu.VMEM((ITERS, NQ, len(PLANE), FR, T), f32),
            pltpu.VMEM((CB, T, S), f32),
            pltpu.VMEM((S, T), f32),
            dma((7,)),
            dma((CB,)),
            dma((ITERS, 2, NQ, 2, 8)),
            dma((ITERS, 2, NQ, 2, 8)),
            dma((ITERS, 2, NQ, 4)),
            dma((ITERS, 2, NQ, 4)),
            dma((ITERS, NQ, 2, len(PLANE))),
            dma((ITERS, NQ, 2, len(PLANE))),
        ],
        compiler_params=pltpu.CompilerParams(
            collective_id=0, has_side_effects=True, vmem_limit_bytes=56 << 20
        ),
        cost_estimate=pl.CostEstimate(
            flops=8 * SLOTS * T * T * S, bytes_accessed=6 << 20, transcendentals=0
        ),
    )(
        inv,
        tile_values,
        unit_cost,
        capacity,
        demand,
        row_kind,
        primal_start,
        dual_start,
    )
    return pl.pallas_call(
        hand_over,
        out_shape=outs,
        in_specs=[hbm] * 2,
        out_specs=(hbm, hbm),
        scratch_shapes=[
            pltpu.VMEM((CB, T, S), f32),
            pltpu.VMEM((RB, T, S), f32),
            dma((CB // 4 + RB // 4,)),
            dma((CB // 4 + RB // 4,)),
        ],
        compiler_params=pltpu.CompilerParams(vmem_limit_bytes=56 << 20),
    )(*results)


def solution(mesh):
    placed = (
        P(("col", "row"), None, None),
        P(("col", "row")),
        P(("col", "row")),
        P("col", None),
        P("col", None),
        P("row", None, None),
        P("row", None),
        P("col", None, None),
        P("row", None, None),
    )
    return jax.shard_map(
        per_device,
        mesh=mesh,
        in_specs=placed,
        out_specs=(P("col", None, None), P("row", None, None)),
        check_vma=False,
    )
```
